32 devices in a mesh: group: 2 (over y), row: 8 (over z, x), col: 2 (over core).
Axes of the slice: x: 2, y: 2, z: 4, core: 2. Of those that a mesh axis runs over, the one named last changes fastest.
Arguments:
- pair: bfloat16 [768, 384, 128], P(('group', 'row'), 'col'), parts along dimension 0, may hold values from -16 to 16
- chain_ids: int32 [768], P('group'), parts along dimension 0, may hold values from 0 to 3, never falling along the last dimension, each value on 1 to 192 neighbouring positions
- token_mask: int32 [768], P('group'), parts along dimension 0, may hold values 0 or 1
- same_chain_bias: bfloat16 [128], replicated, may hold values from -4 to 4
- proj_weight: bfloat16 [2, 128, 512], replicated, may hold values from -0.5 to 0.5
- gate_weight: bfloat16 [2, 128, 128], replicated, may hold values from -0.5 to 0.5
- out_weight: bfloat16 [2, 128, 128], replicated, may hold values from -0.5 to 0.5
Outputs:
- updated: bfloat16 [768, 384, 128], P(('group', 'row'), 'col'), parts along dimension 0
The draws below stay inside these ranges and needn't reach their ends.
There are 2 independent parts, one for each index of `group`. The reference program is written for one: setup_inputs(seed, part) draws one part's arguments, and reference() takes and returns one part's arrays. A program takes and returns all parts, laid end to end along the dimension named above; an argument that names none is the same for every part. Nothing has to cross between parts.
Inputs may be any that keep to these rules, and one draw needn't show every extreme that they name: `chain_ids`: chain ids never fall along the residues.
All inputs are finite; a program needn't handle non-finite values.
Results may differ from the reference program's by a relative error of at most 0.0095.
Values may be sent and summed in bfloat16 or wider, within the bound.
A program may use at most 64 MiB of HBM per device.

```python
import math
import jax
import jax.numpy as jnp
import numpy as np
from jax import lax

C = 128
CH = 128
TOKENS = 384
CHAINS = 4


def draw_pair(key, part):
    key = jax.random.fold_in(key, 11)
    key_base, key_scale = jax.random.split(key)
    scale = jnp.exp(jax.random.uniform(key_scale, (C,), jnp.float32, -1.15, 1.15))
    base = jnp.clip(jax.random.normal(key_base, (TOKENS, TOKENS, C), jnp.float32), -5.0, 5.0)
    return (base * scale[None, None, :]).astype(jnp.bfloat16)


def place_ends(values, own_key, least, largest):
    shape = values.shape
    index_at = [jax.random.randint(jax.random.fold_in(own_key, axis), (), 0, shape[axis]) for axis in range(len(shape))]
    values = values.at[tuple(index_at)].set(least)
    longest = shape.index(max(shape))
    index_at[longest] = (index_at[longest] + 1) % shape[longest]
    return values.at[tuple(index_at)].set(largest)


def profile(number_of, total, limit, skew):
    portions = [(1 << 20) // math.isqrt(rank ** skew) + 1 for rank in range(2, number_of + 1)]
    rest, holding = total - limit - (number_of - 1), [1] * (number_of - 1)
    while rest > 0:
        movable = [i for i in range(number_of - 1) if holding[i] < limit]
        pool, left = sum([portions[i] for i in movable]), rest
        for i in movable:
            extra = min(limit - holding[i], max(1, left * portions[i] // pool), rest)
            holding[i] = holding[i] + extra
            rest = rest - extra
    return np.array([limit] + holding)


def uneven_parts(key, number_of, total, reach, slope):
    if number_of == 2:
        one = jax.random.randint(key, (), max(1, total - reach), min(reach, total - 1) + 1)
        return jnp.stack([one, total - one])
    sizes = jnp.asarray(profile(number_of, total, reach, slope), jnp.int32)
    couples = (number_of - 1) // 2
    donor, receiver = sizes[1:1 + 2 * couples:2], sizes[2:2 + 2 * couples:2]
    slack = jnp.minimum(donor - 1, reach - receiver)
    moved = jax.random.randint(jax.random.fold_in(key, 1), (couples,), 0, 1 << 20) % (slack + 1)
    sizes = sizes.at[1:1 + 2 * couples:2].set(donor - moved).at[2:2 + 2 * couples:2].set(receiver + moved)
    return sizes[jax.random.permutation(jax.random.fold_in(key, 2), number_of)]


def scatter_about(rng, shape, spread, bound, kind=jnp.bfloat16):
    values = spread * jax.random.normal(rng, shape, jnp.float32)
    return jnp.clip(values, min=-bound, max=bound).astype(kind)


def setup_inputs(seed: int = 0, part: int = 0) -> dict:
    streams_of = jax.random.split(jax.random.key(seed), 8)
    own_keys = jax.random.split(jax.random.fold_in(streams_of[7], part), 8)
    pair = draw_pair(jax.random.fold_in(jax.random.fold_in(streams_of[7], part), 71), part)
    chain_ids = jnp.searchsorted(jnp.cumsum(uneven_parts(own_keys[1], CHAINS, TOKENS, TOKENS // 2, 1)), jnp.arange(TOKENS), side="right").astype(jnp.int32)
    token_mask = place_ends((jax.random.randint(own_keys[2], (TOKENS,), 0, 8) < 7).astype(jnp.int32), jax.random.fold_in(own_keys[2], 1), 0, 1)
    same_chain_bias = scatter_about(streams_of[3], (C,), 1.0, 4.0)
    proj_weight = scatter_about(streams_of[4], (2, C, 4 * CH), C ** -0.5, 0.5)
    gate_weight = scatter_about(streams_of[5], (2, C, C), C ** -0.5, 0.5)
    out_weight = scatter_about(streams_of[6], (2, CH, C), CH ** -0.5, 0.5)
    return dict(pair=pair, chain_ids=chain_ids, token_mask=token_mask, same_chain_bias=same_chain_bias, proj_weight=proj_weight, gate_weight=gate_weight, out_weight=out_weight)


def layer_norm(values):
    mean = lax.optimization_barrier(jnp.mean(values, axis=-1, keepdims=True))
    centred = values - mean
    var = lax.optimization_barrier(jnp.mean(centred * centred, axis=-1, keepdims=True))
    return centred * jax.lax.rsqrt(var + 1e-05)

def triangle(pair_now, mask_pair, proj, gate, outw, incoming):
    normed = layer_norm(pair_now.astype(jnp.float32)).astype(jnp.bfloat16)
    flat = normed.reshape(TOKENS * TOKENS, C)
    proj_out = jnp.dot(flat, proj, preferred_element_type=jnp.float32).reshape(TOKENS, TOKENS, 4 * CH)
    masked = mask_pair[:, :, None]
    left = (masked * jax.nn.sigmoid(proj_out[..., CH:2 * CH]) * proj_out[..., 0:CH]).astype(jnp.bfloat16)
    right = (masked * jax.nn.sigmoid(proj_out[..., 3 * CH:4 * CH]) * proj_out[..., 2 * CH:3 * CH]).astype(jnp.bfloat16)
    left32 = left.astype(jnp.float32)
    right32 = right.astype(jnp.float32)
    if incoming:
        tri = jnp.einsum('kic,kjc->ijc', left32, right32)
    else:
        tri = jnp.einsum('ikc,jkc->ijc', left32, right32)
    tri = tri.astype(jnp.bfloat16)
    normed_tri = layer_norm(tri.astype(jnp.float32)).astype(jnp.bfloat16)
    update = jnp.dot(normed_tri.reshape(TOKENS * TOKENS, CH), outw, preferred_element_type=jnp.float32)
    gating = jax.nn.sigmoid(jnp.dot(flat, gate, preferred_element_type=jnp.float32))
    result = pair_now.reshape(TOKENS * TOKENS, C).astype(jnp.float32) + gating * update
    return result.astype(jnp.bfloat16).reshape(TOKENS, TOKENS, C)

def reference(pair, chain_ids, token_mask, same_chain_bias, proj_weight, gate_weight, out_weight):
    same = (chain_ids[:, None] == chain_ids[None, :]).astype(jnp.float32)
    start = (pair.astype(jnp.float32) + same[:, :, None] * same_chain_bias.astype(jnp.float32)[None, None, :]).astype(jnp.bfloat16)
    maskf = token_mask.astype(jnp.float32)
    mask_pair = maskf[:, None] * maskf[None, :]
    first = triangle(start, mask_pair, proj_weight[0], gate_weight[0], out_weight[0], False)
    return triangle(first, mask_pair, proj_weight[1], gate_weight[1], out_weight[1], True)
```

```python
import functools

import jax
import jax.numpy as jnp
from jax import lax
from jax.experimental import pallas as pl
from jax.experimental.pallas import tpu as pltpu
from jax.sharding import PartitionSpec as P

MESH = pl.DeviceIdType.MESH
CHUNKS = 3


def layer_norm(values):
    mean = jnp.mean(values, axis=-1, keepdims=True)
    centred = values - mean
    var = jnp.mean(centred * centred, axis=-1, keepdims=True)
    return centred * lax.rsqrt(var + 1e-05)


def make_contract(rows_grid, cols_grid, rows_tile, cols_tile, incoming):

    def contract(pieces):
        items = pieces.shape[2]
        total = rows_grid * rows_tile
        whole = pieces.reshape(rows_grid, cols_grid, 2, items, rows_tile, cols_tile)
        whole = whole.transpose(2, 3, 0, 4, 1, 5).reshape(2, items, total, cols_grid * cols_tile)
        if incoming:
            tri = jnp.einsum("mki,mkj->mij", whole[0], whole[1], preferred_element_type=jnp.float32)
        else:
            tri = jnp.einsum("mik,mjk->mij", whole[0], whole[1], preferred_element_type=jnp.float32)
        tri = tri.astype(jnp.bfloat16)
        tri = tri.reshape(items, rows_grid, rows_tile, cols_grid, cols_tile).transpose(
            1, 3, 0, 2, 4
        )
        return tri.reshape(rows_grid * cols_grid, items, rows_tile * cols_tile)

    return contract


def triangle(pair_now, mask_flat, proj, gate, outw, incoming):
    rows_tile, cols_tile, channels = pair_now.shape
    hidden = proj.shape[1] // 4
    rows_grid = lax.axis_size("row")
    cols_grid = lax.axis_size("col")
    owners = rows_grid * cols_grid
    per_owner = hidden // owners
    cells = rows_tile * cols_tile
    normed = layer_norm(pair_now.astype(jnp.float32)).astype(jnp.bfloat16).reshape(cells, channels)
    proj_out = jnp.dot(normed, proj, preferred_element_type=jnp.float32)
    left = (
        mask_flat * jax.nn.sigmoid(proj_out[:, hidden : 2 * hidden]) * proj_out[:, 0:hidden]
    ).astype(jnp.bfloat16)
    right = (
        mask_flat
        * jax.nn.sigmoid(proj_out[:, 3 * hidden : 4 * hidden])
        * proj_out[:, 2 * hidden : 3 * hidden]
    ).astype(jnp.bfloat16)
    stacked = jnp.stack([left, right]).reshape(2, cells, owners, per_owner).transpose(2, 0, 3, 1)
    contract = make_contract(rows_grid, cols_grid, rows_tile, cols_tile, incoming)
    result = contract(
        lax.all_to_all(stacked, ("row", "col"), split_axis=0, concat_axis=0, tiled=True)
    )
    returned = lax.all_to_all(result, ("row", "col"), split_axis=0, concat_axis=0, tiled=True)
    tri = returned.reshape(hidden, cells).T
    normed_tri = layer_norm(tri.astype(jnp.float32)).astype(jnp.bfloat16)
    update = jnp.dot(normed_tri, outw, preferred_element_type=jnp.float32)
    gating = jax.nn.sigmoid(jnp.dot(normed, gate, preferred_element_type=jnp.float32))
    result_flat = pair_now.reshape(cells, channels).astype(jnp.float32) + gating * update
    return result_flat.astype(jnp.bfloat16).reshape(rows_tile, cols_tile, channels)


def shards(pair, chain_ids, token_mask, same_chain_bias, proj_weight, gate_weight, out_weight):
    rows_tile, cols_tile, channels = pair.shape
    row_index = lax.axis_index("row")
    col_index = lax.axis_index("col")
    row_start = row_index * rows_tile
    col_start = col_index * cols_tile
    chain_rows = lax.dynamic_slice_in_dim(chain_ids, row_start, rows_tile)
    chain_cols = lax.dynamic_slice_in_dim(chain_ids, col_start, cols_tile)
    mask_rows = lax.dynamic_slice_in_dim(token_mask, row_start, rows_tile).astype(jnp.float32)
    mask_cols = lax.dynamic_slice_in_dim(token_mask, col_start, cols_tile).astype(jnp.float32)
    same = (chain_rows[:, None] == chain_cols[None, :]).astype(jnp.float32)
    start = (
        pair.astype(jnp.float32)
        + same[:, :, None] * same_chain_bias.astype(jnp.float32)[None, None, :]
    ).astype(jnp.bfloat16)
    mask_flat = (mask_rows[:, None] * mask_cols[None, :]).reshape(rows_tile * cols_tile, 1)
    first = triangle(start, mask_flat, proj_weight[0], gate_weight[0], out_weight[0], False)
    return triangle(first, mask_flat, proj_weight[1], gate_weight[1], out_weight[1], True)


def sigmoid(values):
    return 0.5 * jnp.tanh(0.5 * values) + 0.5


def normalise(values, axis):
    mean = jnp.mean(values, axis=axis, keepdims=True)
    centred = values - mean
    var = jnp.mean(centred * centred, axis=axis, keepdims=True)
    return (centred * lax.rsqrt(var + 1e-05)).astype(jnp.bfloat16)


def fused_kernel(
    rows_grid,
    pair_ref,
    chain_s,
    mask_s,
    chain_v,
    mask_v,
    bias_v,
    proj_v,
    gate_v,
    outw_v,
    out_ref,
    cells,
    normed,
    outbox,
    inbox,
    wide,
    products,
    back_out,
    back_in,
    pair_sems,
    fwd_send,
    fwd_recv,
    back_send,
    back_recv,
    own_sems,
    out_sems,
):
    owners = 2 * rows_grid
    rows, tokens, _ = cells.shape
    half = tokens // 2
    per = inbox.shape[1] // 2
    step_rows = rows // CHUNKS
    tiles = tokens // 128
    row, col = lax.axis_index("row"), lax.axis_index("col")
    me = row * 2 + col
    sibling = {"row": row, "col": 1 - col}
    mine = pl.multiple_of(col * half, half)
    theirs = pl.multiple_of((1 - col) * half, half)

    def place(owner):
        return {"row": owner // 2, "col": owner % 2}

    barrier = pltpu.get_barrier_semaphore()

    def greet(step, carry):
        pl.semaphore_signal(
            barrier, inc=1, device_id=place((me + step) % owners), device_id_type=MESH
        )
        return carry

    lax.fori_loop(1, owners, greet, 0)
    pl.semaphore_wait(barrier, owners - 1)

    keep = pltpu.make_async_copy(
        pair_ref.at[pl.ds(col * rows, rows)], cells.at[:, pl.ds(mine, half)], pair_sems.at[0]
    )
    swap = pltpu.make_async_remote_copy(
        src_ref=pair_ref.at[pl.ds((1 - col) * rows, rows)],
        dst_ref=cells.at[:, pl.ds(mine, half)],
        send_sem=pair_sems.at[1],
        recv_sem=pair_sems.at[2],
        device_id=sibling,
        device_id_type=MESH,
    )
    keep.start()
    swap.start()
    keep.wait()
    swap.wait()

    def fwd_copy(chunk, owner, source):
        return pltpu.make_async_remote_copy(
            src_ref=outbox.at[owner, pl.ds(chunk * step_rows, step_rows)],
            dst_ref=inbox.at[pl.ds(source * rows + chunk * step_rows, step_rows)],
            send_sem=fwd_send.at[chunk, owner],
            recv_sem=fwd_recv.at[chunk, source],
            device_id=place(owner),
            device_id_type=MESH,
        )

    def fwd_own(chunk):
        return pltpu.make_async_copy(
            outbox.at[me, pl.ds(chunk * step_rows, step_rows)],
            inbox.at[pl.ds(me * rows + chunk * step_rows, step_rows)],
            own_sems.at[0, chunk],
        )

    back_rows = step_rows * per

    def back_copy(chunk, target, source):
        return pltpu.make_async_remote_copy(
            src_ref=back_out.at[target, pl.ds(chunk * back_rows, back_rows)],
            dst_ref=back_in.at[source, pl.ds(chunk * back_rows, back_rows)],
            send_sem=back_send.at[chunk, target],
            recv_sem=back_recv.at[chunk, source],
            device_id=place(target),
            device_id_type=MESH,
        )

    def back_own(chunk):
        return pltpu.make_async_copy(
            back_out.at[me, pl.ds(chunk * back_rows, back_rows)],
            back_in.at[me, pl.ds(chunk * back_rows, back_rows)],
            own_sems.at[1, chunk],
        )

    def produce(update, chunk):
        def one_row(step, carry):
            at = chunk * step_rows + step
            token = row * (2 * rows) + col * rows + at
            values = cells[at].astype(jnp.float32)
            if update == 0:
                same = chain_v[...] == chain_s[token]
                start = (values + jnp.where(same, bias_v[...], 0.0)).astype(jnp.bfloat16)
                cells[at] = start
                values = start.astype(jnp.float32)
            flat = normalise(values, 1)
            normed[at] = flat
            proj = lax.dot_general(
                proj_v[update],
                flat,
                (((1,), (1,)), ((), ())),
                preferred_element_type=jnp.float32,
            )
            width = proj.shape[0] // 2
            mask = mask_s[token] * mask_v[...]
            gated = (mask * sigmoid(proj[width:]) * proj[:width]).astype(jnp.bfloat16)
            outbox[:, at] = gated.reshape(owners, 2 * per, tokens)
            return carry

        lax.fori_loop(0, step_rows, one_row, 0)
        fwd_own(chunk).start()

        def send(step, carry):
            fwd_copy(chunk, (me + step) % owners, me).start()
            return carry

        lax.fori_loop(1, owners, send, 0)

    def contract(update):
        def widen(chunk, source):
            first = source * rows + chunk * step_rows
            block = inbox[pl.ds(first, step_rows)].astype(jnp.float32)
            base = pl.multiple_of(first * (2 * per), 2 * per)
            block = block.reshape(-1, tokens)
            for tile in range(tiles):
                wide[tile, pl.ds(base, step_rows * 2 * per), :] = block[
                    :, tile * 128 : (tile + 1) * 128
                ]

        for chunk in range(CHUNKS):
            fwd_own(chunk).wait()
            widen(chunk, me)

            def arrive(step, carry):
                source = (me + owners - step) % owners
                fwd_copy(chunk, me, source).wait_recv()
                widen(chunk, source)
                return carry

            lax.fori_loop(1, owners, arrive, 0)

        axis = 0 if update == 1 else 1

        def channel(index, carry):
            def pick(first):
                pieces = [
                    wide[tile, pl.ds(first, tokens, stride=2 * per), :].astype(jnp.bfloat16)
                    for tile in range(tiles)
                ]
                return jnp.concatenate(pieces, axis=1)

            left, right = pick(index), pick(per + index)
            tri = lax.dot_general(
                left, right, (((axis,), (axis,)), ((), ())), preferred_element_type=jnp.float32
            )
            for tile in range(tiles):
                products[tile, pl.ds(index, tokens, stride=per), :] = tri[
                    :, tile * 128 : (tile + 1) * 128
                ]
            return carry

        lax.fori_loop(0, per, channel, 0)

        def sent(chunk):
            def one(step, carry):
                fwd_copy(chunk, (me + step) % owners, me).wait_send()
                return carry

            lax.fori_loop(1, owners, one, 0)

        for chunk in range(CHUNKS):

            def pack(target):
                base = pl.multiple_of((target * rows + chunk * step_rows) * per, back_rows)
                block = jnp.concatenate(
                    [products[tile, pl.ds(base, back_rows), :] for tile in range(tiles)], axis=1
                )
                back_out[target, pl.ds(chunk * back_rows, back_rows)] = block.astype(jnp.bfloat16)

            def give(step, carry):
                target = (me + step) % owners
                pack(target)
                back_copy(chunk, target, me).start()
                return carry

            lax.fori_loop(1, owners, give, 0)
            pack(me)
            back_own(chunk).start()
        for chunk in range(CHUNKS):
            sent(chunk)

    def consume(update, chunk):
        def arrive(step, carry):
            back_copy(chunk, me, (me + owners - step) % owners).wait_recv()
            return carry

        lax.fori_loop(1, owners, arrive, 0)
        back_own(chunk).wait()

        def two_rows(step, carry):
            base = pl.multiple_of(chunk * back_rows + step * (2 * per), 2 * per)
            both = back_in[:, pl.ds(base, 2 * per), :].astype(jnp.float32)
            for which in range(2):
                at = chunk * step_rows + 2 * step + which
                tri = both[:, which * per : (which + 1) * per].reshape(owners * per, tokens)
                flat_tri = normalise(tri, 0)
                change = lax.dot_general(
                    flat_tri,
                    outw_v[update],
                    (((0,), (0,)), ((), ())),
                    preferred_element_type=jnp.float32,
                )
                gating = sigmoid(
                    jnp.dot(normed[at], gate_v[update], preferred_element_type=jnp.float32)
                )
                values = cells[at].astype(jnp.float32) + gating * change
                cells[at] = values.astype(jnp.bfloat16)
            return carry

        lax.fori_loop(0, step_rows // 2, two_rows, 0)

    def returned():
        for chunk in range(CHUNKS):

            def one(step, carry):
                back_copy(chunk, (me + step) % owners, me).wait_send()
                return carry

            lax.fori_loop(1, owners, one, 0)

    def results(chunk):
        at = pl.ds(chunk * step_rows, step_rows)
        to = pl.ds(col * rows + chunk * step_rows, step_rows)
        own = pltpu.make_async_copy(
            cells.at[at, pl.ds(mine, half)], out_ref.at[to], out_sems.at[0, chunk]
        )
        other = pltpu.make_async_remote_copy(
            src_ref=cells.at[at, pl.ds(theirs, half)],
            dst_ref=out_ref.at[to],
            send_sem=out_sems.at[1, chunk],
            recv_sem=out_sems.at[2, chunk],
            device_id=sibling,
            device_id_type=MESH,
        )
        return own, other

    for chunk in range(CHUNKS):
        produce(0, chunk)
    contract(0)
    for chunk in range(CHUNKS):
        consume(0, chunk)
        produce(1, chunk)
    returned()
    contract(1)
    for chunk in range(CHUNKS):
        consume(1, chunk)
        for copy in results(chunk):
            copy.start()
    returned()
    for chunk in range(CHUNKS):
        for copy in results(chunk):
            copy.wait()


def fused_shards(
    pair, chain_ids, token_mask, same_chain_bias, proj_weight, gate_weight, out_weight
):
    rows_tile, cols_tile, channels = pair.shape
    rows_grid = lax.axis_size("row")
    owners = 2 * rows_grid
    tokens = 2 * cols_tile
    rows = rows_tile // 2
    hidden = proj_weight.shape[2] // 4
    per = hidden // owners
    parts = proj_weight.reshape(2, channels, 2, 2, owners, per)
    proj = parts.transpose(0, 3, 4, 2, 5, 1).reshape(2, 4 * hidden, channels)
    chain_cols = jnp.broadcast_to(chain_ids[:, None], (tokens, channels))
    mask = token_mask.astype(jnp.float32)
    bf16, f32 = jnp.bfloat16, jnp.float32
    vmem = pl.BlockSpec(memory_space=pltpu.VMEM)
    smem = pl.BlockSpec(memory_space=pltpu.SMEM)
    anywhere = pl.BlockSpec(memory_space=pl.ANY)
    return pl.pallas_call(
        functools.partial(fused_kernel, rows_grid),
        out_shape=jax.ShapeDtypeStruct(pair.shape, pair.dtype),
        in_specs=[anywhere, smem, smem, vmem, vmem, vmem, vmem, vmem, vmem],
        out_specs=anywhere,
        scratch_shapes=[
            pltpu.VMEM((rows, tokens, channels), bf16),
            pltpu.VMEM((rows, tokens, channels), bf16),
            pltpu.VMEM((owners, rows, 2 * per, tokens), bf16),
            pltpu.VMEM((tokens, 2 * per, tokens), bf16),
            pltpu.VMEM((tokens // 128, tokens * 2 * per, 128), f32),
            pltpu.VMEM((tokens // 128, tokens * per, 128), f32),
            pltpu.VMEM((owners, rows * per, tokens), bf16),
            pltpu.VMEM((owners, rows * per, tokens), bf16),
            pltpu.SemaphoreType.DMA((3,)),
            pltpu.SemaphoreType.DMA((CHUNKS, owners)),
            pltpu.SemaphoreType.DMA((CHUNKS, owners)),
            pltpu.SemaphoreType.DMA((CHUNKS, owners)),
            pltpu.SemaphoreType.DMA((CHUNKS, owners)),
            pltpu.SemaphoreType.DMA((2, CHUNKS)),
            pltpu.SemaphoreType.DMA((3, CHUNKS)),
        ],
        compiler_params=pltpu.CompilerParams(
            collective_id=0, has_side_effects=True, vmem_limit_bytes=56 * 1024 * 1024
        ),
    )(
        pair,
        chain_ids,
        mask,
        chain_cols,
        mask[None, :],
        same_chain_bias.astype(f32)[None, :],
        proj,
        gate_weight,
        out_weight,
    )


def fits(pair, proj_weight):
    rows_tile, cols_tile, channels = pair.shape
    rows_grid, cols_grid = lax.axis_size("row"), lax.axis_size("col")
    hidden = proj_weight.shape[2] // 4
    return (
        cols_grid == 2
        and hidden == 8 * cols_grid * rows_grid
        and channels == 128
        and rows_tile % (4 * CHUNKS) == 0
        and cols_tile % 64 == 0
        and (2 * cols_tile) % 128 == 0
        and rows_tile * rows_grid == cols_tile * cols_grid
    )


def program_shards(pair, chain_ids, token_mask, same_chain_bias, proj_weight, *rest):
    chosen = fused_shards if fits(pair, proj_weight) else shards
    return chosen(pair, chain_ids, token_mask, same_chain_bias, proj_weight, *rest)


def solution(mesh):
    return jax.shard_map(
        program_shards,
        mesh=mesh,
        in_specs=(P(("group", "row"), "col", None), P("group"), P("group"), P(), P(), P(), P()),
        out_specs=P(("group", "row"), "col", None),
        check_vma=False,
    )
```

```python
import functools

import jax
import jax.numpy as jnp
from jax import lax
from jax.experimental import pallas as pl
from jax.experimental.pallas import tpu as pltpu
from jax.sharding import PartitionSpec as P

MESH = pl.DeviceIdType.MESH
CHUNKS = 3


def layer_norm(values):
    mean = jnp.mean(values, axis=-1, keepdims=True)
    centred = values - mean
    var = jnp.mean(centred * centred, axis=-1, keepdims=True)
    return centred * lax.rsqrt(var + 1e-05)


def make_contract(rows_grid, cols_grid, rows_tile, cols_tile, incoming):

    def contract(pieces):
        items = pieces.shape[2]
        total = rows_grid * rows_tile
        whole = pieces.reshape(rows_grid, cols_grid, 2, items, rows_tile, cols_tile)
        whole = whole.transpose(2, 3, 0, 4, 1, 5).reshape(2, items, total, cols_grid * cols_tile)
        if incoming:
            tri = jnp.einsum("mki,mkj->mij", whole[0], whole[1], preferred_element_type=jnp.float32)
        else:
            tri = jnp.einsum("mik,mjk->mij", whole[0], whole[1], preferred_element_type=jnp.float32)
        tri = tri.astype(jnp.bfloat16)
        tri = tri.reshape(items, rows_grid, rows_tile, cols_grid, cols_tile).transpose(
            1, 3, 0, 2, 4
        )
        return tri.reshape(rows_grid * cols_grid, items, rows_tile * cols_tile)

    return contract


def triangle(pair_now, mask_flat, proj, gate, outw, incoming):
    rows_tile, cols_tile, channels = pair_now.shape
    hidden = proj.shape[1] // 4
    rows_grid = lax.axis_size("row")
    cols_grid = lax.axis_size("col")
    owners = rows_grid * cols_grid
    per_owner = hidden // owners
    cells = rows_tile * cols_tile
    normed = layer_norm(pair_now.astype(jnp.float32)).astype(jnp.bfloat16).reshape(cells, channels)
    proj_out = jnp.dot(normed, proj, preferred_element_type=jnp.float32)
    left = (
        mask_flat * jax.nn.sigmoid(proj_out[:, hidden : 2 * hidden]) * proj_out[:, 0:hidden]
    ).astype(jnp.bfloat16)
    right = (
        mask_flat
        * jax.nn.sigmoid(proj_out[:, 3 * hidden : 4 * hidden])
        * proj_out[:, 2 * hidden : 3 * hidden]
    ).astype(jnp.bfloat16)
    stacked = jnp.stack([left, right]).reshape(2, cells, owners, per_owner).transpose(2, 0, 3, 1)
    contract = make_contract(rows_grid, cols_grid, rows_tile, cols_tile, incoming)
    result = contract(
        lax.all_to_all(stacked, ("row", "col"), split_axis=0, concat_axis=0, tiled=True)
    )
    returned = lax.all_to_all(result, ("row", "col"), split_axis=0, concat_axis=0, tiled=True)
    tri = returned.reshape(hidden, cells).T
    normed_tri = layer_norm(tri.astype(jnp.float32)).astype(jnp.bfloat16)
    update = jnp.dot(normed_tri, outw, preferred_element_type=jnp.float32)
    gating = jax.nn.sigmoid(jnp.dot(normed, gate, preferred_element_type=jnp.float32))
    result_flat = pair_now.reshape(cells, channels).astype(jnp.float32) + gating * update
    return result_flat.astype(jnp.bfloat16).reshape(rows_tile, cols_tile, channels)


def shards(pair, chain_ids, token_mask, same_chain_bias, proj_weight, gate_weight, out_weight):
    rows_tile, cols_tile, channels = pair.shape
    row_index = lax.axis_index("row")
    col_index = lax.axis_index("col")
    row_start = row_index * rows_tile
    col_start = col_index * cols_tile
    chain_rows = lax.dynamic_slice_in_dim(chain_ids, row_start, rows_tile)
    chain_cols = lax.dynamic_slice_in_dim(chain_ids, col_start, cols_tile)
    mask_rows = lax.dynamic_slice_in_dim(token_mask, row_start, rows_tile).astype(jnp.float32)
    mask_cols = lax.dynamic_slice_in_dim(token_mask, col_start, cols_tile).astype(jnp.float32)
    same = (chain_rows[:, None] == chain_cols[None, :]).astype(jnp.float32)
    start = (
        pair.astype(jnp.float32)
        + same[:, :, None] * same_chain_bias.astype(jnp.float32)[None, None, :]
    ).astype(jnp.bfloat16)
    mask_flat = (mask_rows[:, None] * mask_cols[None, :]).reshape(rows_tile * cols_tile, 1)
    first = triangle(start, mask_flat, proj_weight[0], gate_weight[0], out_weight[0], False)
    return triangle(first, mask_flat, proj_weight[1], gate_weight[1], out_weight[1], True)


def sigmoid(values):
    return 0.5 * jnp.tanh(0.5 * values) + 0.5


def normalise(values, axis):
    mean = jnp.mean(values, axis=axis, keepdims=True)
    centred = values - mean
    var = jnp.mean(centred * centred, axis=axis, keepdims=True)
    return (centred * lax.rsqrt(var + 1e-05)).astype(jnp.bfloat16)


def fused_kernel(
    rows_grid,
    pair_ref,
    chain_s,
    mask_s,
    chain_v,
    mask_v,
    bias_v,
    proj_v,
    gate_v,
    outw_v,
    out_ref,
    cells,
    normed,
    outbox,
    left_in,
    right_in,
    inbox,
    wide,
    products,
    back_out,
    back_in,
    pair_sems,
    left_send,
    left_recv,
    right_send,
    right_recv,
    fwd_send,
    fwd_recv,
    back_send,
    back_recv,
    own_sems,
    out_sems,
):
    owners = 2 * rows_grid
    team = owners // 2
    rows, tokens, _ = cells.shape
    half = tokens // 2
    per = inbox.shape[1] // 2
    wide_per = 2 * per
    step_rows = rows // CHUNKS
    tiles = tokens // 128
    row, col = lax.axis_index("row"), lax.axis_index("col")
    me = row * 2 + col
    seat = me % team
    base_team = me - seat
    other_team = team - base_team
    sibling = {"row": row, "col": 1 - col}
    mine = pl.multiple_of(col * half, half)
    theirs = pl.multiple_of((1 - col) * half, half)

    def place(owner):
        return {"row": owner // 2, "col": owner % 2}

    barrier = pltpu.get_barrier_semaphore()

    def greet(step, carry):
        pl.semaphore_signal(
            barrier, inc=1, device_id=place((me + step) % owners), device_id_type=MESH
        )
        return carry

    lax.fori_loop(1, owners, greet, 0)
    pl.semaphore_wait(barrier, owners - 1)

    keep = pltpu.make_async_copy(
        pair_ref.at[pl.ds(col * rows, rows)], cells.at[:, pl.ds(mine, half)], pair_sems.at[0]
    )
    swap = pltpu.make_async_remote_copy(
        src_ref=pair_ref.at[pl.ds((1 - col) * rows, rows)],
        dst_ref=cells.at[:, pl.ds(mine, half)],
        send_sem=pair_sems.at[1],
        recv_sem=pair_sems.at[2],
        device_id=sibling,
        device_id_type=MESH,
    )
    keep.start()
    swap.start()
    keep.wait()
    swap.wait()

    def part(chunk):
        return pl.ds(chunk * step_rows, step_rows)

    def left_copy(chunk, target, source):
        return pltpu.make_async_remote_copy(
            src_ref=outbox.at[target, part(chunk), pl.ds(0, wide_per)],
            dst_ref=left_in.at[pl.ds(source * rows + chunk * step_rows, step_rows)],
            send_sem=left_send.at[chunk, target],
            recv_sem=left_recv.at[chunk, source],
            device_id=place(base_team + target),
            device_id_type=MESH,
        )

    def left_own(chunk):
        return pltpu.make_async_copy(
            outbox.at[seat, part(chunk), pl.ds(0, wide_per)],
            left_in.at[pl.ds(seat * rows + chunk * step_rows, step_rows)],
            own_sems.at[0, chunk],
        )

    def right_copy(chunk, target, source):
        return pltpu.make_async_remote_copy(
            src_ref=outbox.at[target % team, part(chunk), pl.ds(wide_per, wide_per)],
            dst_ref=right_in.at[pl.ds(source * rows + chunk * step_rows, step_rows)],
            send_sem=right_send.at[chunk, target],
            recv_sem=right_recv.at[chunk, source],
            device_id=place(target),
            device_id_type=MESH,
        )

    def right_own(chunk):
        return pltpu.make_async_copy(
            outbox.at[seat, part(chunk), pl.ds(wide_per, wide_per)],
            right_in.at[pl.ds(me * rows + chunk * step_rows, step_rows)],
            own_sems.at[1, chunk],
        )

    def share(owner):
        return pl.ds(pl.multiple_of((owner % 2) * wide_per, wide_per), wide_per)

    def fwd_copy(chunk, owner, source):
        return pltpu.make_async_remote_copy(
            src_ref=outbox.at[owner // 2, part(chunk), share(owner)],
            dst_ref=inbox.at[pl.ds(source * rows + chunk * step_rows, step_rows)],
            send_sem=fwd_send.at[chunk, owner],
            recv_sem=fwd_recv.at[chunk, source],
            device_id=place(owner),
            device_id_type=MESH,
        )

    def fwd_own(chunk):
        return pltpu.make_async_copy(
            outbox.at[me // 2, part(chunk), share(me)],
            inbox.at[pl.ds(me * rows + chunk * step_rows, step_rows)],
            own_sems.at[2, chunk],
        )

    def back_view(ref, update, chunk, owner):
        if update == 0:
            size = step_rows * wide_per
            return ref.at[owner, pl.ds(chunk * size, size)]
        size = step_rows * per
        first = pl.multiple_of((owner % 2) * (rows * per) + chunk * size, size)
        return ref.at[owner // 2, pl.ds(first, size)]

    def back_copy(update, chunk, target, source):
        return pltpu.make_async_remote_copy(
            src_ref=back_view(back_out, update, chunk, target),
            dst_ref=back_view(back_in, update, chunk, source),
            send_sem=back_send.at[chunk, target],
            recv_sem=back_recv.at[chunk, source],
            device_id=place(target + base_team if update == 0 else target),
            device_id_type=MESH,
        )

    def back_own(update, chunk):
        at = seat if update == 0 else me
        return pltpu.make_async_copy(
            back_view(back_out, update, chunk, at),
            back_view(back_in, update, chunk, at),
            own_sems.at[3, chunk],
        )

    def each(first, last, act):
        def body(step, carry):
            act(step)
            return carry

        lax.fori_loop(first, last, body, 0)

    def send_first(chunk):
        def act(step):
            near = (seat + step) % team
            right_copy(chunk, other_team + near, me).start()
            right_copy(chunk, base_team + near, me).start()
            left_copy(chunk, near, seat).start()

        left_own(chunk).start()
        right_own(chunk).start()
        right_copy(chunk, other_team + seat, me).start()
        each(1, team, act)

    def sent_first(chunk):
        def act(step):
            near = (seat + step) % team
            right_copy(chunk, other_team + near, me).wait_send()
            right_copy(chunk, base_team + near, me).wait_send()
            left_copy(chunk, near, seat).wait_send()

        right_copy(chunk, other_team + seat, me).wait_send()
        each(1, team, act)

    def send_second(chunk):
        fwd_own(chunk).start()
        each(1, owners, lambda step: fwd_copy(chunk, (me + step) % owners, me).start())

    def sent_second(chunk):
        each(1, owners, lambda step: fwd_copy(chunk, (me + step) % owners, me).wait_send())

    def produce(update, chunk):
        def one_row(step):
            at = chunk * step_rows + step
            token = me * rows + at
            values = cells[at].astype(jnp.float32)
            if update == 0:
                same = chain_v[...] == chain_s[token]
                start = (values + jnp.where(same, bias_v[...], 0.0)).astype(jnp.bfloat16)
                cells[at] = start
                values = start.astype(jnp.float32)
            flat = normalise(values, 1)
            normed[at] = flat
            proj = lax.dot_general(
                proj_v[update],
                flat,
                (((1,), (1,)), ((), ())),
                preferred_element_type=jnp.float32,
            )
            width = proj.shape[0] // 2
            mask = mask_s[token] * mask_v[...]
            gated = (mask * sigmoid(proj[width:]) * proj[:width]).astype(jnp.bfloat16)
            outbox[:, at] = gated.reshape(team, 2 * wide_per, tokens)

        each(0, step_rows, one_row)
        if update == 0:
            send_first(chunk)
        else:
            send_second(chunk)

    def widen(box, chunk, source, offset):
        first = source * rows + chunk * step_rows
        block = box[pl.ds(first, step_rows)].astype(jnp.float32).reshape(-1, tokens)
        base = pl.multiple_of(offset + first * wide_per, wide_per)
        for tile in range(tiles):
            wide[tile, pl.ds(base, step_rows * wide_per), :] = block[
                :, tile * 128 : (tile + 1) * 128
            ]

    def pick(first, size):
        pieces = [
            wide[tile, pl.ds(first, size, stride=wide_per), :].astype(jnp.bfloat16)
            for tile in range(tiles)
        ]
        return jnp.concatenate(pieces, axis=1)

    def keep_product(tri, index, count):
        size = tri.shape[0]
        for tile in range(tiles):
            products[tile, pl.ds(index, size, stride=count), :] = tri[
                :, tile * 128 : (tile + 1) * 128
            ]

    def give_back(update, count, people, own):
        for chunk in range(CHUNKS):
            size = step_rows * count

            def pack(target):
                base = pl.multiple_of((target * rows + chunk * step_rows) * count, size)
                block = jnp.concatenate(
                    [products[tile, pl.ds(base, size), :] for tile in range(tiles)], axis=1
                )
                back_view(back_out, update, chunk, target)[...] = block.astype(jnp.bfloat16)

            def give(step):
                target = (own + step) % people
                pack(target)
                back_copy(update, chunk, target, own).start()

            each(1, people, give)
            pack(own)
            back_own(update, chunk).start()

    def contract_first():
        team_rows = team * rows
        offset = team_rows * wide_per
        for chunk in range(CHUNKS):
            left_own(chunk).wait()
            right_own(chunk).wait()
            widen(left_in, chunk, seat, 0)
            widen(right_in, chunk, me, offset)

            def arrive(step):
                near = (seat + team - step) % team
                right_copy(chunk, me, other_team + near).wait_recv()
                widen(right_in, chunk, other_team + near, offset)
                right_copy(chunk, me, base_team + near).wait_recv()
                widen(right_in, chunk, base_team + near, offset)
                left_copy(chunk, seat, near).wait_recv()
                widen(left_in, chunk, near, 0)

            right_copy(chunk, me, other_team + seat).wait_recv()
            widen(right_in, chunk, other_team + seat, offset)
            each(1, team, arrive)

        def channel(index):
            left = pick(index, team_rows)
            right = pick(offset + index, tokens)
            tri = lax.dot_general(
                left, right, (((1,), (1,)), ((), ())), preferred_element_type=jnp.float32
            )
            keep_product(tri, index, wide_per)

        each(0, wide_per, channel)
        give_back(0, wide_per, team, seat)
        for chunk in range(CHUNKS):
            sent_first(chunk)

    def contract_second():
        for chunk in range(CHUNKS):
            fwd_own(chunk).wait()
            widen(inbox, chunk, me, 0)

            def arrive(step):
                source = (me + owners - step) % owners
                fwd_copy(chunk, me, source).wait_recv()
                widen(inbox, chunk, source, 0)

            each(1, owners, arrive)

        def channel(index):
            left = pick(index, tokens)
            right = pick(per + index, tokens)
            tri = lax.dot_general(
                left, right, (((0,), (0,)), ((), ())), preferred_element_type=jnp.float32
            )
            keep_product(tri, index, per)

        each(0, per, channel)
        give_back(1, per, owners, me)
        for chunk in range(CHUNKS):
            sent_second(chunk)

    def finish(update, at, tri):
        flat_tri = normalise(tri, 0)
        change = lax.dot_general(
            flat_tri, outw_v[update], (((0,), (0,)), ((), ())), preferred_element_type=jnp.float32
        )
        gating = sigmoid(jnp.dot(normed[at], gate_v[update], preferred_element_type=jnp.float32))
        cells[at] = (cells[at].astype(jnp.float32) + gating * change).astype(jnp.bfloat16)

    def consume_first(chunk):
        each(
            1,
            team,
            lambda step: back_copy(0, chunk, seat, (seat + team - step) % team).wait_recv(),
        )
        back_own(0, chunk).wait()

        def one_row(step):
            at = chunk * step_rows + step
            base = pl.multiple_of(at * wide_per, wide_per)
            tri = back_in[:, pl.ds(base, wide_per), :].astype(jnp.float32)
            finish(0, at, tri.reshape(owners * per, tokens))

        each(0, step_rows, one_row)

    def consume_second(chunk):
        each(
            1,
            owners,
            lambda step: back_copy(1, chunk, me, (me + owners - step) % owners).wait_recv(),
        )
        back_own(1, chunk).wait()

        def two_rows(step):
            at = chunk * step_rows + 2 * step
            base = pl.multiple_of(at * per, wide_per)
            even = back_in[:, pl.ds(base, wide_per), :].astype(jnp.float32)
            odd = back_in[:, pl.ds(rows * per + base, wide_per), :].astype(jnp.float32)
            for which in range(2):
                lanes = slice(which * per, (which + 1) * per)
                tri = jnp.concatenate([even[:, lanes], odd[:, lanes]], axis=1)
                finish(1, at + which, tri.reshape(owners * per, tokens))

        each(0, step_rows // 2, two_rows)

    def returned(update, people, own):
        for chunk in range(CHUNKS):
            each(
                1,
                people,
                lambda step: back_copy(update, chunk, (own + step) % people, own).wait_send(),
            )

    def results(chunk):
        at = part(chunk)
        to = pl.ds(col * rows + chunk * step_rows, step_rows)
        own = pltpu.make_async_copy(
            cells.at[at, pl.ds(mine, half)], out_ref.at[to], out_sems.at[0, chunk]
        )
        other = pltpu.make_async_remote_copy(
            src_ref=cells.at[at, pl.ds(theirs, half)],
            dst_ref=out_ref.at[to],
            send_sem=out_sems.at[1, chunk],
            recv_sem=out_sems.at[2, chunk],
            device_id=sibling,
            device_id_type=MESH,
        )
        return own, other

    for chunk in range(CHUNKS):
        produce(0, chunk)
    contract_first()
    for chunk in range(CHUNKS):
        consume_first(chunk)
        produce(1, chunk)
    returned(0, team, seat)
    contract_second()
    for chunk in range(CHUNKS):
        consume_second(chunk)
        for copy in results(chunk):
            copy.start()
    returned(1, owners, me)
    for chunk in range(CHUNKS):
        for copy in results(chunk):
            copy.wait()


def arrange(weight, groups):
    channels, width = weight.shape
    parts = weight.reshape(channels, 2, 2, groups, width // (4 * groups))
    return parts.transpose(2, 3, 1, 4, 0).reshape(width, channels)


def fused_shards(
    pair, chain_ids, token_mask, same_chain_bias, proj_weight, gate_weight, out_weight
):
    rows_tile, cols_tile, channels = pair.shape
    rows_grid = lax.axis_size("row")
    owners = 2 * rows_grid
    team = owners // 2
    tokens = 2 * cols_tile
    rows = rows_tile // 2
    hidden = proj_weight.shape[2] // 4
    per = hidden // owners
    proj = jnp.stack([arrange(proj_weight[0], team), arrange(proj_weight[1], owners)])
    chain_cols = jnp.broadcast_to(chain_ids[:, None], (tokens, channels))
    mask = token_mask.astype(jnp.float32)
    bf16, f32 = jnp.bfloat16, jnp.float32
    vmem = pl.BlockSpec(memory_space=pltpu.VMEM)
    smem = pl.BlockSpec(memory_space=pltpu.SMEM)
    anywhere = pl.BlockSpec(memory_space=pl.ANY)

    def sems(*shape):
        return pltpu.SemaphoreType.DMA(shape)

    return pl.pallas_call(
        functools.partial(fused_kernel, rows_grid),
        out_shape=jax.ShapeDtypeStruct(pair.shape, pair.dtype),
        in_specs=[anywhere, smem, smem, vmem, vmem, vmem, vmem, vmem, vmem],
        out_specs=anywhere,
        scratch_shapes=[
            pltpu.VMEM((rows, tokens, channels), bf16),
            pltpu.VMEM((rows, tokens, channels), bf16),
            pltpu.VMEM((team, rows, 4 * per, tokens), bf16),
            pltpu.VMEM((team * rows, 2 * per, tokens), bf16),
            pltpu.VMEM((tokens, 2 * per, tokens), bf16),
            pltpu.VMEM((tokens, 2 * per, tokens), bf16),
            pltpu.VMEM((tokens // 128, (tokens + team * rows) * 2 * per, 128), f32),
            pltpu.VMEM((tokens // 128, tokens * per, 128), f32),
            pltpu.VMEM((team, rows * 2 * per, tokens), bf16),
            pltpu.VMEM((team, rows * 2 * per, tokens), bf16),
            sems(3),
            sems(CHUNKS, team),
            sems(CHUNKS, team),
            sems(CHUNKS, owners),
            sems(CHUNKS, owners),
            sems(CHUNKS, owners),
            sems(CHUNKS, owners),
            sems(CHUNKS, owners),
            sems(CHUNKS, owners),
            sems(4, CHUNKS),
            sems(3, CHUNKS),
        ],
        compiler_params=pltpu.CompilerParams(
            collective_id=0, has_side_effects=True, vmem_limit_bytes=60 * 1024 * 1024
        ),
    )(
        pair,
        chain_ids,
        mask,
        chain_cols,
        mask[None, :],
        same_chain_bias.astype(f32)[None, :],
        proj,
        gate_weight,
        out_weight,
    )


def fits(pair, proj_weight):
    rows_tile, cols_tile, channels = pair.shape
    rows_grid, cols_grid = lax.axis_size("row"), lax.axis_size("col")
    hidden = proj_weight.shape[2] // 4
    return (
        cols_grid == 2
        and rows_grid % 2 == 0
        and hidden == 8 * cols_grid * rows_grid
        and channels == 128
        and rows_tile % (4 * CHUNKS) == 0
        and cols_tile % 64 == 0
        and (2 * cols_tile) % 128 == 0
        and rows_tile * rows_grid == cols_tile * cols_grid
    )


def program_shards(pair, chain_ids, token_mask, same_chain_bias, proj_weight, *rest):
    chosen = fused_shards if fits(pair, proj_weight) else shards
    return chosen(pair, chain_ids, token_mask, same_chain_bias, proj_weight, *rest)


def solution(mesh):
    return jax.shard_map(
        program_shards,
        mesh=mesh,
        in_specs=(P(("group", "row"), "col", None), P("group"), P("group"), P(), P(), P(), P()),
        out_specs=P(("group", "row"), "col", None),
        check_vma=False,
    )
```

```python
import functools

import jax
import jax.numpy as jnp
from jax import lax
from jax.experimental import pallas as pl
from jax.experimental.pallas import tpu as pltpu
from jax.sharding import PartitionSpec as P

MESH = pl.DeviceIdType.MESH
CHUNKS = 3


def layer_norm(values):
    mean = jnp.mean(values, axis=-1, keepdims=True)
    centred = values - mean
    var = jnp.mean(centred * centred, axis=-1, keepdims=True)
    return centred * lax.rsqrt(var + 1e-05)


def make_contract(rows_grid, cols_grid, rows_tile, cols_tile, incoming):

    def contract(pieces):
        items = pieces.shape[2]
        total = rows_grid * rows_tile
        whole = pieces.reshape(rows_grid, cols_grid, 2, items, rows_tile, cols_tile)
        whole = whole.transpose(2, 3, 0, 4, 1, 5).reshape(2, items, total, cols_grid * cols_tile)
        if incoming:
            tri = jnp.einsum("mki,mkj->mij", whole[0], whole[1], preferred_element_type=jnp.float32)
        else:
            tri = jnp.einsum("mik,mjk->mij", whole[0], whole[1], preferred_element_type=jnp.float32)
        tri = tri.astype(jnp.bfloat16)
        tri = tri.reshape(items, rows_grid, rows_tile, cols_grid, cols_tile).transpose(
            1, 3, 0, 2, 4
        )
        return tri.reshape(rows_grid * cols_grid, items, rows_tile * cols_tile)

    return contract


def triangle(pair_now, mask_flat, proj, gate, outw, incoming):
    rows_tile, cols_tile, channels = pair_now.shape
    hidden = proj.shape[1] // 4
    rows_grid = lax.axis_size("row")
    cols_grid = lax.axis_size("col")
    owners = rows_grid * cols_grid
    per_owner = hidden // owners
    cells = rows_tile * cols_tile
    normed = layer_norm(pair_now.astype(jnp.float32)).astype(jnp.bfloat16).reshape(cells, channels)
    proj_out = jnp.dot(normed, proj, preferred_element_type=jnp.float32)
    left = (
        mask_flat * jax.nn.sigmoid(proj_out[:, hidden : 2 * hidden]) * proj_out[:, 0:hidden]
    ).astype(jnp.bfloat16)
    right = (
        mask_flat
        * jax.nn.sigmoid(proj_out[:, 3 * hidden : 4 * hidden])
        * proj_out[:, 2 * hidden : 3 * hidden]
    ).astype(jnp.bfloat16)
    stacked = jnp.stack([left, right]).reshape(2, cells, owners, per_owner).transpose(2, 0, 3, 1)
    contract = make_contract(rows_grid, cols_grid, rows_tile, cols_tile, incoming)
    result = contract(
        lax.all_to_all(stacked, ("row", "col"), split_axis=0, concat_axis=0, tiled=True)
    )
    returned = lax.all_to_all(result, ("row", "col"), split_axis=0, concat_axis=0, tiled=True)
    tri = returned.reshape(hidden, cells).T
    normed_tri = layer_norm(tri.astype(jnp.float32)).astype(jnp.bfloat16)
    update = jnp.dot(normed_tri, outw, preferred_element_type=jnp.float32)
    gating = jax.nn.sigmoid(jnp.dot(normed, gate, preferred_element_type=jnp.float32))
    result_flat = pair_now.reshape(cells, channels).astype(jnp.float32) + gating * update
    return result_flat.astype(jnp.bfloat16).reshape(rows_tile, cols_tile, channels)


def shards(pair, chain_ids, token_mask, same_chain_bias, proj_weight, gate_weight, out_weight):
    rows_tile, cols_tile, channels = pair.shape
    row_index = lax.axis_index("row")
    col_index = lax.axis_index("col")
    row_start = row_index * rows_tile
    col_start = col_index * cols_tile
    chain_rows = lax.dynamic_slice_in_dim(chain_ids, row_start, rows_tile)
    chain_cols = lax.dynamic_slice_in_dim(chain_ids, col_start, cols_tile)
    mask_rows = lax.dynamic_slice_in_dim(token_mask, row_start, rows_tile).astype(jnp.float32)
    mask_cols = lax.dynamic_slice_in_dim(token_mask, col_start, cols_tile).astype(jnp.float32)
    same = (chain_rows[:, None] == chain_cols[None, :]).astype(jnp.float32)
    start = (
        pair.astype(jnp.float32)
        + same[:, :, None] * same_chain_bias.astype(jnp.float32)[None, None, :]
    ).astype(jnp.bfloat16)
    mask_flat = (mask_rows[:, None] * mask_cols[None, :]).reshape(rows_tile * cols_tile, 1)
    first = triangle(start, mask_flat, proj_weight[0], gate_weight[0], out_weight[0], False)
    return triangle(first, mask_flat, proj_weight[1], gate_weight[1], out_weight[1], True)


def sigmoid(values):
    return 0.5 * jnp.tanh(0.5 * values) + 0.5


def normalise(values, axis):
    mean = jnp.mean(values, axis=axis, keepdims=True)
    centred = values - mean
    var = jnp.mean(centred * centred, axis=axis, keepdims=True)
    return (centred * lax.rsqrt(var + 1e-05)).astype(jnp.bfloat16)


def fused_kernel(
    rows_grid,
    pair_ref,
    chain_s,
    mask_s,
    chain_v,
    mask_v,
    bias_v,
    proj_v,
    gate_v,
    outw_v,
    out_ref,
    cells,
    normed,
    first_out,
    left_in,
    right_in,
    wide,
    products,
    back_out,
    back_in,
    second_out,
    second_in,
    others,
    cross_out,
    cross_in,
    last_out,
    last_in,
    pair_sems,
    left_send,
    left_recv,
    right_send,
    right_recv,
    back_send,
    back_recv,
    second_send,
    second_recv,
    cross_send,
    cross_recv,
    last_send,
    last_recv,
    own_sems,
    last_own,
    out_sems,
):
    owners = 2 * rows_grid
    team = owners // 2
    rows, tiles, chips, pair_rows, channels = cells.shape
    step_rows = rows // CHUNKS
    lanes = chips * pair_rows
    tokens = tiles * lanes
    per = left_in.shape[1]
    team_rows = team * rows
    batch = 4
    row, col = lax.axis_index("row"), lax.axis_index("col")
    me = row * 2 + col
    seat = me % team
    base_team = me - seat
    other_team = team - base_team
    sibling = {"row": row, "col": 1 - col}
    half_chips = chips // 2

    def place(owner):
        return {"row": owner // 2, "col": owner % 2}

    def each(first, last, act):
        def body(step, carry):
            act(step)
            return carry

        lax.fori_loop(first, last, body, 0)

    barrier = pltpu.get_barrier_semaphore()

    def greet(step):
        pl.semaphore_signal(
            barrier, inc=1, device_id=place((me + step) % owners), device_id_type=MESH
        )

    each(1, owners, greet)
    pl.semaphore_wait(barrier, owners - 1)

    def part(chunk):
        return pl.ds(chunk * step_rows, step_rows)

    def tile_rows(chunk, core):
        return pl.ds(chunk * (2 * step_rows) + core * step_rows, step_rows)

    def pair_copies(chunk, tile):
        into = cells.at[part(chunk), tile, pl.ds(col * half_chips, half_chips)]
        own = pltpu.make_async_copy(
            pair_ref.at[tile_rows(chunk, col), :, tile], into, pair_sems.at[0, chunk, tile]
        )
        other = pltpu.make_async_remote_copy(
            src_ref=pair_ref.at[tile_rows(chunk, 1 - col), :, tile],
            dst_ref=into,
            send_sem=pair_sems.at[1, chunk, tile],
            recv_sem=pair_sems.at[2, chunk, tile],
            device_id=sibling,
            device_id_type=MESH,
        )
        return own, other

    def out_copies(chunk, tile):
        to = out_ref.at[tile_rows(chunk, col), :, tile]
        own = pltpu.make_async_copy(
            cells.at[part(chunk), tile, pl.ds(col * half_chips, half_chips)],
            to,
            out_sems.at[0, chunk, tile],
        )
        other = pltpu.make_async_remote_copy(
            src_ref=cells.at[part(chunk), tile, pl.ds((1 - col) * half_chips, half_chips)],
            dst_ref=to,
            send_sem=out_sems.at[1, chunk, tile],
            recv_sem=out_sems.at[2, chunk, tile],
            device_id=sibling,
            device_id_type=MESH,
        )
        return own, other

    def left_copy(chunk, target, source):
        return pltpu.make_async_remote_copy(
            src_ref=first_out.at[target, part(chunk), pl.ds(0, per)],
            dst_ref=left_in.at[pl.ds(source * rows + chunk * step_rows, step_rows)],
            send_sem=left_send.at[chunk, target],
            recv_sem=left_recv.at[chunk, source],
            device_id=place(base_team + target),
            device_id_type=MESH,
        )

    def left_own(chunk):
        return pltpu.make_async_copy(
            first_out.at[seat, part(chunk), pl.ds(0, per)],
            left_in.at[pl.ds(seat * rows + chunk * step_rows, step_rows)],
            own_sems.at[0, chunk],
        )

    def right_copy(chunk, target, source):
        return pltpu.make_async_remote_copy(
            src_ref=first_out.at[target % team, part(chunk), pl.ds(per, per)],
            dst_ref=right_in.at[chunk, pl.ds(source * step_rows, step_rows)],
            send_sem=right_send.at[chunk, target],
            recv_sem=right_recv.at[chunk, source],
            device_id=place(target),
            device_id_type=MESH,
        )

    def right_own(chunk):
        return pltpu.make_async_copy(
            first_out.at[seat, part(chunk), pl.ds(per, per)],
            right_in.at[chunk, pl.ds(me * step_rows, step_rows)],
            own_sems.at[1, chunk],
        )

    def team_copy(out_box, in_box, send, recv, index, target, source):
        return pltpu.make_async_remote_copy(
            src_ref=out_box.at[index, target],
            dst_ref=in_box.at[index, source],
            send_sem=send.at[index, target],
            recv_sem=recv.at[index, source],
            device_id=place(base_team + target),
            device_id_type=MESH,
        )

    back_copy = functools.partial(team_copy, back_out, back_in, back_send, back_recv)
    second_copy = functools.partial(team_copy, second_out, second_in, second_send, second_recv)
    last_copy = functools.partial(team_copy, last_out, last_in, last_send, last_recv)

    def back_own(tile):
        return pltpu.make_async_copy(
            back_out.at[tile, seat], back_in.at[tile, seat], own_sems.at[2, tile]
        )

    def second_own(tile):
        return pltpu.make_async_copy(
            second_out.at[tile, seat], second_in.at[tile, seat], own_sems.at[3, tile]
        )

    def last_own_copy(block):
        return pltpu.make_async_copy(
            last_out.at[block, seat], last_in.at[block, seat], last_own.at[block]
        )

    def cross_copy(block):
        return pltpu.make_async_remote_copy(
            src_ref=cross_out.at[block],
            dst_ref=cross_in.at[block],
            send_sem=cross_send.at[block],
            recv_sem=cross_recv.at[block],
            device_id=place(other_team + seat),
            device_id_type=MESH,
        )

    def near(step):
        return (seat + step) % team

    def send_left(chunk):
        left_own(chunk).start()
        each(1, team, lambda step: left_copy(chunk, near(step), seat).start())

    def send_right(chunk):
        def act(step):
            right_copy(chunk, other_team + near(step), me).start()
            right_copy(chunk, base_team + near(step), me).start()

        right_own(chunk).start()
        right_copy(chunk, other_team + seat, me).start()
        each(1, team, act)

    def project(update, flat):
        proj = lax.dot_general(
            proj_v[update], flat, (((1,), (1,)), ((), ())), preferred_element_type=jnp.float32
        )
        width = proj.shape[0] // 2
        return sigmoid(proj[width:]) * proj[:width]

    def mask_at(at):
        chunk, step = at // step_rows, at % step_rows
        return row * (2 * rows) + chunk * (2 * step_rows) + col * step_rows + step

    def produce_first(chunk):
        def one_row(step):
            at = chunk * step_rows + step
            token = mask_at(at)
            values = cells[at].reshape(tokens, channels).astype(jnp.float32)
            same = chain_v[...] == chain_s[token]
            start = (values + jnp.where(same, bias_v[...], 0.0)).astype(jnp.bfloat16)
            cells[at] = start.reshape(tiles, chips, pair_rows, channels)
            flat = normalise(start.astype(jnp.float32), 1)
            normed[at] = flat.reshape(tiles, lanes, channels)
            gated = (mask_s[token] * mask_v[...]) * project(0, flat)
            first_out[:, at] = gated.astype(jnp.bfloat16).reshape(team, 2 * per, tokens)

        each(0, step_rows, one_row)

    def widen(block, base):
        block = block.astype(jnp.float32).reshape(-1, block.shape[-1])
        size = block.shape[0]
        for tile in range(block.shape[1] // lanes):
            wide[tile, pl.ds(base, size), :] = block[:, tile * lanes : (tile + 1) * lanes]

    def pick(first, size, stride):
        pieces = [
            wide[tile, pl.ds(first, size, stride=stride), :].astype(jnp.bfloat16)
            for tile in range(tiles)
        ]
        return jnp.concatenate(pieces, axis=1)

    right_base = team_rows * per

    def widen_left(chunk, source):
        first = source * rows + chunk * step_rows
        widen(left_in[pl.ds(first, step_rows)], pl.multiple_of(first * per, per))

    def widen_right(chunk, source):
        first = source * step_rows
        base = pl.multiple_of(right_base + first * per, per)
        widen(right_in[chunk, pl.ds(first, step_rows)], base)

    def take_left():
        for chunk in range(CHUNKS):
            left_own(chunk).wait()
            widen_left(chunk, seat)

            def arrive(step):
                source = (seat + team - step) % team
                left_copy(chunk, seat, source).wait_recv()
                widen_left(chunk, source)

            each(1, team, arrive)

    def take_right(chunk):
        def arrive(step):
            source = (me + owners - step) % owners
            right_copy(chunk, me, source).wait_recv()
            widen_right(chunk, source)

        right_own(chunk).wait()
        widen_right(chunk, me)
        each(1, owners, arrive)

    def contract_first(tile):
        def channel(index):
            left = pick(index, team_rows, per)
            right = pick(right_base + index, lanes, per)
            tri = lax.dot_general(
                left, right, (((1,), (1,)), ((), ())), preferred_element_type=jnp.float32
            )
            products[pl.ds(index, team_rows, stride=per), :] = tri

        each(0, per, channel)
        size = rows * per

        def give(step):
            target = near(step)
            base = pl.multiple_of(target * size, size)
            back_out[tile, target] = products[pl.ds(base, size), :].astype(jnp.bfloat16)

            @pl.when(step > 0)
            def _():
                back_copy(tile, target, seat).start()

        each(0, team, give)
        back_own(tile).start()

    def finish(update, at, tile, tris):
        tri = jnp.concatenate(tris, axis=1)
        here = pl.ds(at, batch)
        change = lax.dot_general(
            normalise(tri, 0),
            outw_v[update],
            (((0,), (0,)), ((), ())),
            preferred_element_type=jnp.float32,
        )
        flat = normed[here, tile].reshape(batch * lanes, channels)
        gating = sigmoid(jnp.dot(flat, gate_v[update], preferred_element_type=jnp.float32))
        values = cells[here, tile].reshape(batch * lanes, channels).astype(jnp.float32)
        result = (values + gating * change).astype(jnp.bfloat16)
        cells[here, tile] = result.reshape(batch, chips, pair_rows, channels)
        return result

    def team_arrived(copy, index):
        each(1, team, lambda step: copy(index, seat, (seat + team - step) % team).wait_recv())

    def consume_first(tile):
        team_arrived(back_copy, tile)
        back_own(tile).wait()
        mask_tile = mask_v[:, tile * lanes : (tile + 1) * lanes]

        def some_rows(step):
            at = step * batch
            tris = []
            for which in range(batch):
                base = pl.multiple_of((at + which) * per, per)
                tri = back_in[tile, :, pl.ds(base, per), :].astype(jnp.float32)
                tris.append(tri.reshape(team * per, lanes))
            result = finish(0, at, tile, tris)
            flat = normalise(result.astype(jnp.float32), 1)
            normed[pl.ds(at, batch), tile] = flat.reshape(batch, lanes, channels)
            gated = project(1, flat)
            for which in range(batch):
                mask = mask_s[mask_at(at + which)] * mask_tile
                piece = (mask * gated[:, which * lanes : (which + 1) * lanes]).astype(jnp.bfloat16)
                second_out[tile, :, at + which] = piece.reshape(team, 2 * per, lanes)

        each(0, rows // batch, some_rows)
        second_own(tile).start()
        each(1, team, lambda step: second_copy(tile, near(step), seat).start())

    def take_second(tile):
        def put(source):
            size = rows * 2 * per
            block = second_in[tile, source].astype(jnp.float32).reshape(size, lanes)
            wide[tile, pl.ds(pl.multiple_of(source * size, size), size), :] = block

        def arrive(step):
            source = (seat + team - step) % team
            second_copy(tile, seat, source).wait_recv()
            put(source)

        second_own(tile).wait()
        put(seat)
        each(1, team, arrive)

    block_rows = team * step_rows
    block_size = block_rows * per
    blocks = []
    for newest in range(CHUNKS):
        for older in range(newest):
            blocks += [(older, newest), (newest, older)]
        blocks.append((newest, newest))

    def partial_block(block):
        chunk, tile = blocks[block]
        stride = 2 * per

        def channel(index):
            left = wide[chunk, pl.ds(index, team_rows, stride=stride), :]
            right = wide[tile, pl.ds(per + index, team_rows, stride=stride), :]
            tri = lax.dot_general(
                left.astype(jnp.bfloat16),
                right.astype(jnp.bfloat16),
                (((0,), (0,)), ((), ())),
                preferred_element_type=jnp.float32,
            )
            low, high = tri[:block_rows], tri[block_rows:]
            lower = base_team == 0
            products[pl.ds(block * block_size + index, block_rows, stride=per), :] = jnp.where(
                lower, low, high
            )
            others[pl.ds(index, block_rows, stride=per), :] = jnp.where(lower, high, low)

        each(0, per, channel)
        cross_out[block] = others[...].astype(jnp.bfloat16)
        cross_copy(block).start()

    def combine(block):
        cross_copy(block).wait_recv()
        size = step_rows * per

        def give(step):
            target = near(step)
            first = pl.multiple_of(target * size, size)
            total = products[pl.ds(block * block_size + first, size), :] + cross_in[
                block, pl.ds(first, size), :
            ].astype(jnp.float32)
            last_out[block, target] = total.astype(jnp.bfloat16)

            @pl.when(step > 0)
            def _():
                last_copy(block, target, seat).start()

        each(0, team, give)
        last_own_copy(block).start()

    def consume_second(block):
        chunk, tile = blocks[block]
        team_arrived(last_copy, block)
        last_own_copy(block).wait()
        for first in range(0, step_rows, batch):
            tris = []
            for which in range(first, first + batch):
                tri = last_in[block, :, which * per : (which + 1) * per, :].astype(jnp.float32)
                tris.append(tri.reshape(team * per, lanes))
            finish(1, chunk * step_rows + first, tile, tris)
        for copy in out_copies(chunk, tile):
            copy.start()

    grid = [(chunk, tile) for chunk in range(CHUNKS) for tile in range(tiles)]
    for at in grid:
        for copy in pair_copies(*at):
            copy.start()
    for chunk in range(CHUNKS):
        for tile in range(tiles):
            for copy in pair_copies(chunk, tile):
                copy.wait()
        produce_first(chunk)
        if chunk == 0:
            send_right(0)
        send_left(chunk)
    for chunk in range(1, CHUNKS):
        send_right(chunk)
    take_left()
    for tile in range(tiles):
        take_right(tile)
        contract_first(tile)
        if tile:
            consume_first(tile - 1)
    take_second(0)
    partial_block(0)
    consume_first(tiles - 1)
    done = 1
    for tile in range(1, tiles):
        take_second(tile)
        while done < (tile + 1) ** 2:
            partial_block(done)
            done += 1
    for block in range(len(blocks)):
        combine(block)
        if block:
            consume_second(block - 1)
    consume_second(len(blocks) - 1)

    for chunk in range(CHUNKS):

        def sent(step):
            left_copy(chunk, near(step), seat).wait_send()
            right_copy(chunk, other_team + near(step), me).wait_send()
            right_copy(chunk, base_team + near(step), me).wait_send()
            back_copy(chunk, near(step), seat).wait_send()
            second_copy(chunk, near(step), seat).wait_send()

        right_copy(chunk, other_team + seat, me).wait_send()
        each(1, team, sent)
    for block in range(len(blocks)):
        cross_copy(block).wait_send()
        each(1, team, lambda step: last_copy(block, near(step), seat).wait_send())
    for at in grid:
        for copy in out_copies(*at):
            copy.wait()


def arrange(weight, groups):
    channels, width = weight.shape
    parts = weight.reshape(channels, 2, 2, groups, width // (4 * groups))
    return parts.transpose(2, 3, 1, 4, 0).reshape(width, channels)


def fused_shards(
    pair, chain_ids, token_mask, same_chain_bias, proj_weight, gate_weight, out_weight
):
    rows_tile, cols_tile, channels = pair.shape
    chips = lax.axis_size("row")
    owners = 2 * chips
    team = owners // 2
    tokens = 2 * cols_tile
    rows = rows_tile // 2
    step_rows = rows // CHUNKS
    hidden = proj_weight.shape[2] // 4
    per = hidden // team
    lanes = owners * step_rows
    blocks = CHUNKS * CHUNKS
    proj = jnp.stack([arrange(proj_weight[t], team) for t in range(2)])

    def dealt(values):
        parts = values.reshape(chips, CHUNKS, 2 * step_rows)
        return parts.transpose(1, 0, 2).reshape(tokens)

    chain_cols = jnp.broadcast_to(dealt(chain_ids)[:, None], (tokens, channels))
    mask = token_mask.astype(jnp.float32)
    bf16, f32 = jnp.bfloat16, jnp.float32
    vmem = pl.BlockSpec(memory_space=pltpu.VMEM)
    smem = pl.BlockSpec(memory_space=pltpu.SMEM)
    anywhere = pl.BlockSpec(memory_space=pl.ANY)
    view = (rows_tile, chips // 2, CHUNKS, 2 * step_rows, channels)

    def sems(*shape):
        return pltpu.SemaphoreType.DMA(shape)

    result = pl.pallas_call(
        functools.partial(fused_kernel, chips),
        out_shape=jax.ShapeDtypeStruct(view, pair.dtype),
        in_specs=[anywhere, smem, smem, vmem, vmem, vmem, vmem, vmem, vmem],
        out_specs=anywhere,
        scratch_shapes=[
            pltpu.VMEM((rows, CHUNKS, chips, 2 * step_rows, channels), bf16),
            pltpu.VMEM((rows, CHUNKS, lanes, channels), bf16),
            pltpu.VMEM((team, rows, 2 * per, tokens), bf16),
            pltpu.VMEM((team * rows, per, tokens), bf16),
            pltpu.VMEM((CHUNKS, lanes, per, tokens), bf16),
            pltpu.VMEM((CHUNKS, team * rows * 2 * per, lanes), f32),
            pltpu.VMEM((blocks * team * step_rows * per, lanes), f32),
            pltpu.VMEM((CHUNKS, team, rows * per, lanes), bf16),
            pltpu.VMEM((CHUNKS, team, rows * per, lanes), bf16),
            pltpu.VMEM((CHUNKS, team, rows, 2 * per, lanes), bf16),
            pltpu.VMEM((CHUNKS, team, rows, 2 * per, lanes), bf16),
            pltpu.VMEM((team * step_rows * per, lanes), f32),
            pltpu.VMEM((blocks, team * step_rows * per, lanes), bf16),
            pltpu.VMEM((blocks, team * step_rows * per, lanes), bf16),
            pltpu.VMEM((blocks, team, step_rows * per, lanes), bf16),
            pltpu.VMEM((blocks, team, step_rows * per, lanes), bf16),
            sems(3, CHUNKS, CHUNKS),
            sems(CHUNKS, team),
            sems(CHUNKS, team),
            sems(CHUNKS, owners),
            sems(CHUNKS, owners),
            sems(CHUNKS, team),
            sems(CHUNKS, team),
            sems(CHUNKS, team),
            sems(CHUNKS, team),
            sems(blocks),
            sems(blocks),
            sems(blocks, team),
            sems(blocks, team),
            sems(4, CHUNKS),
            sems(blocks),
            sems(3, CHUNKS, CHUNKS),
        ],
        compiler_params=pltpu.CompilerParams(
            collective_id=0, has_side_effects=True, vmem_limit_bytes=60 * 1024 * 1024
        ),
    )(
        pair.reshape(view),
        chain_ids,
        mask,
        chain_cols,
        dealt(mask)[None, :],
        same_chain_bias.astype(f32)[None, :],
        proj,
        gate_weight,
        out_weight,
    )
    return result.reshape(pair.shape)


def fits(pair, proj_weight):
    rows_tile, cols_tile, channels = pair.shape
    rows_grid, cols_grid = lax.axis_size("row"), lax.axis_size("col")
    hidden = proj_weight.shape[2] // 4
    return (
        cols_grid == 2
        and rows_grid % 2 == 0
        and hidden == 8 * cols_grid * rows_grid
        and channels == 128
        and rows_tile % (4 * CHUNKS) == 0
        and cols_tile % 64 == 0
        and rows_tile * rows_grid == 128 * CHUNKS
        and rows_tile * rows_grid == cols_tile * cols_grid
    )


def program_shards(pair, chain_ids, token_mask, same_chain_bias, proj_weight, *rest):
    chosen = fused_shards if fits(pair, proj_weight) else shards
    return chosen(pair, chain_ids, token_mask, same_chain_bias, proj_weight, *rest)


def solution(mesh):
    return jax.shard_map(
        program_shards,
        mesh=mesh,
        in_specs=(P(("group", "row"), "col", None), P("group"), P("group"), P(), P(), P(), P()),
        out_specs=P(("group", "row"), "col", None),
        check_vma=False,
    )
```

```python
import functools

import jax
import jax.numpy as jnp
from jax import lax
from jax.experimental import pallas as pl
from jax.experimental.pallas import tpu as pltpu
from jax.sharding import PartitionSpec as P

MESH = pl.DeviceIdType.MESH
CHUNKS = 3


def layer_norm(values):
    mean = jnp.mean(values, axis=-1, keepdims=True)
    centred = values - mean
    var = jnp.mean(centred * centred, axis=-1, keepdims=True)
    return centred * lax.rsqrt(var + 1e-05)


def make_contract(rows_grid, cols_grid, rows_tile, cols_tile, incoming):

    def contract(pieces):
        items = pieces.shape[2]
        total = rows_grid * rows_tile
        whole = pieces.reshape(rows_grid, cols_grid, 2, items, rows_tile, cols_tile)
        whole = whole.transpose(2, 3, 0, 4, 1, 5).reshape(2, items, total, cols_grid * cols_tile)
        if incoming:
            tri = jnp.einsum("mki,mkj->mij", whole[0], whole[1], preferred_element_type=jnp.float32)
        else:
            tri = jnp.einsum("mik,mjk->mij", whole[0], whole[1], preferred_element_type=jnp.float32)
        tri = tri.astype(jnp.bfloat16)
        tri = tri.reshape(items, rows_grid, rows_tile, cols_grid, cols_tile).transpose(
            1, 3, 0, 2, 4
        )
        return tri.reshape(rows_grid * cols_grid, items, rows_tile * cols_tile)

    return contract


def triangle(pair_now, mask_flat, proj, gate, outw, incoming):
    rows_tile, cols_tile, channels = pair_now.shape
    hidden = proj.shape[1] // 4
    rows_grid = lax.axis_size("row")
    cols_grid = lax.axis_size("col")
    owners = rows_grid * cols_grid
    per_owner = hidden // owners
    cells = rows_tile * cols_tile
    normed = layer_norm(pair_now.astype(jnp.float32)).astype(jnp.bfloat16).reshape(cells, channels)
    proj_out = jnp.dot(normed, proj, preferred_element_type=jnp.float32)
    left = (
        mask_flat * jax.nn.sigmoid(proj_out[:, hidden : 2 * hidden]) * proj_out[:, 0:hidden]
    ).astype(jnp.bfloat16)
    right = (
        mask_flat
        * jax.nn.sigmoid(proj_out[:, 3 * hidden : 4 * hidden])
        * proj_out[:, 2 * hidden : 3 * hidden]
    ).astype(jnp.bfloat16)
    stacked = jnp.stack([left, right]).reshape(2, cells, owners, per_owner).transpose(2, 0, 3, 1)
    contract = make_contract(rows_grid, cols_grid, rows_tile, cols_tile, incoming)
    result = contract(
        lax.all_to_all(stacked, ("row", "col"), split_axis=0, concat_axis=0, tiled=True)
    )
    returned = lax.all_to_all(result, ("row", "col"), split_axis=0, concat_axis=0, tiled=True)
    tri = returned.reshape(hidden, cells).T
    normed_tri = layer_norm(tri.astype(jnp.float32)).astype(jnp.bfloat16)
    update = jnp.dot(normed_tri, outw, preferred_element_type=jnp.float32)
    gating = jax.nn.sigmoid(jnp.dot(normed, gate, preferred_element_type=jnp.float32))
    result_flat = pair_now.reshape(cells, channels).astype(jnp.float32) + gating * update
    return result_flat.astype(jnp.bfloat16).reshape(rows_tile, cols_tile, channels)


def shards(pair, chain_ids, token_mask, same_chain_bias, proj_weight, gate_weight, out_weight):
    rows_tile, cols_tile, channels = pair.shape
    row_index = lax.axis_index("row")
    col_index = lax.axis_index("col")
    row_start = row_index * rows_tile
    col_start = col_index * cols_tile
    chain_rows = lax.dynamic_slice_in_dim(chain_ids, row_start, rows_tile)
    chain_cols = lax.dynamic_slice_in_dim(chain_ids, col_start, cols_tile)
    mask_rows = lax.dynamic_slice_in_dim(token_mask, row_start, rows_tile).astype(jnp.float32)
    mask_cols = lax.dynamic_slice_in_dim(token_mask, col_start, cols_tile).astype(jnp.float32)
    same = (chain_rows[:, None] == chain_cols[None, :]).astype(jnp.float32)
    start = (
        pair.astype(jnp.float32)
        + same[:, :, None] * same_chain_bias.astype(jnp.float32)[None, None, :]
    ).astype(jnp.bfloat16)
    mask_flat = (mask_rows[:, None] * mask_cols[None, :]).reshape(rows_tile * cols_tile, 1)
    first = triangle(start, mask_flat, proj_weight[0], gate_weight[0], out_weight[0], False)
    return triangle(first, mask_flat, proj_weight[1], gate_weight[1], out_weight[1], True)


def sigmoid(values):
    return 0.5 * jnp.tanh(0.5 * values) + 0.5


def normalise(values, axis):
    mean = jnp.mean(values, axis=axis, keepdims=True)
    centred = values - mean
    var = jnp.mean(centred * centred, axis=axis, keepdims=True)
    return (centred * lax.rsqrt(var + 1e-05)).astype(jnp.bfloat16)


def block_order():
    blocks, groups = [], []
    for newest in range(CHUNKS):
        first = len(blocks)
        for older in range(newest):
            blocks += [(older, newest), (newest, older)]
        blocks.append((newest, newest))
        cut = first + (len(blocks) - first) // 2 if newest == CHUNKS - 1 else len(blocks)
        groups.append((first, cut, newest))
        if cut < len(blocks):
            groups.append((cut, len(blocks), newest))
    return blocks, groups


def fused_kernel(
    rows_grid,
    pair_ref,
    chain_s,
    mask_s,
    chain_v,
    mask_v,
    bias_v,
    proj_v,
    gate_v,
    outw_v,
    out_ref,
    cells,
    normed,
    first_out,
    left_in,
    right_in,
    wide,
    products,
    back_out,
    back_in,
    second_out,
    second_in,
    last_out,
    last_in,
    pair_sems,
    left_send,
    left_recv,
    right_send,
    right_recv,
    back_send,
    back_recv,
    second_send,
    second_recv,
    last_send,
    last_recv,
    own_sems,
    last_own,
    out_sems,
):
    owners = 2 * rows_grid
    team = owners // 2
    rows, tiles, chips, pair_rows, channels = cells.shape
    step_rows = rows // CHUNKS
    lanes = chips * pair_rows
    tokens = tiles * lanes
    per = left_in.shape[1]
    team_rows = team * rows
    batch = 4
    row, col = lax.axis_index("row"), lax.axis_index("col")
    me = row * 2 + col
    seat = me % team
    base_team = me - seat
    other_team = team - base_team
    sibling = {"row": row, "col": 1 - col}
    half_chips = chips // 2
    share = team * per // owners
    blocks, groups = block_order()

    def place(owner):
        return {"row": owner // 2, "col": owner % 2}

    def each(first, last, act):
        def body(step, carry):
            act(step)
            return carry

        lax.fori_loop(first, last, body, 0)

    barrier = pltpu.get_barrier_semaphore()

    def greet(step):
        pl.semaphore_signal(
            barrier, inc=1, device_id=place((me + step) % owners), device_id_type=MESH
        )

    each(1, owners, greet)
    pl.semaphore_wait(barrier, owners - 1)

    def part(chunk):
        return pl.ds(chunk * step_rows, step_rows)

    def tile_rows(chunk, core):
        return pl.ds(chunk * (2 * step_rows) + core * step_rows, step_rows)

    def pair_copies(chunk, tile):
        into = cells.at[part(chunk), tile, pl.ds(col * half_chips, half_chips)]
        own = pltpu.make_async_copy(
            pair_ref.at[tile_rows(chunk, col), :, tile], into, pair_sems.at[0, chunk, tile]
        )
        other = pltpu.make_async_remote_copy(
            src_ref=pair_ref.at[tile_rows(chunk, 1 - col), :, tile],
            dst_ref=into,
            send_sem=pair_sems.at[1, chunk, tile],
            recv_sem=pair_sems.at[2, chunk, tile],
            device_id=sibling,
            device_id_type=MESH,
        )
        return own, other

    def out_copies(chunk, tile):
        to = out_ref.at[tile_rows(chunk, col), :, tile]
        own = pltpu.make_async_copy(
            cells.at[part(chunk), tile, pl.ds(col * half_chips, half_chips)],
            to,
            out_sems.at[0, chunk, tile],
        )
        other = pltpu.make_async_remote_copy(
            src_ref=cells.at[part(chunk), tile, pl.ds((1 - col) * half_chips, half_chips)],
            dst_ref=to,
            send_sem=out_sems.at[1, chunk, tile],
            recv_sem=out_sems.at[2, chunk, tile],
            device_id=sibling,
            device_id_type=MESH,
        )
        return own, other

    def left_copy(chunk, target, source):
        return pltpu.make_async_remote_copy(
            src_ref=first_out.at[target, part(chunk), pl.ds(0, per)],
            dst_ref=left_in.at[pl.ds(source * rows + chunk * step_rows, step_rows)],
            send_sem=left_send.at[chunk, target],
            recv_sem=left_recv.at[chunk, source],
            device_id=place(base_team + target),
            device_id_type=MESH,
        )

    def left_own(chunk):
        return pltpu.make_async_copy(
            first_out.at[seat, part(chunk), pl.ds(0, per)],
            left_in.at[pl.ds(seat * rows + chunk * step_rows, step_rows)],
            own_sems.at[0, chunk],
        )

    def right_copy(chunk, target, source):
        return pltpu.make_async_remote_copy(
            src_ref=first_out.at[target % team, part(chunk), pl.ds(per, per)],
            dst_ref=right_in.at[chunk, pl.ds(source * step_rows, step_rows)],
            send_sem=right_send.at[chunk, target],
            recv_sem=right_recv.at[chunk, source],
            device_id=place(target),
            device_id_type=MESH,
        )

    def right_own(chunk):
        return pltpu.make_async_copy(
            first_out.at[seat, part(chunk), pl.ds(per, per)],
            right_in.at[chunk, pl.ds(me * step_rows, step_rows)],
            own_sems.at[1, chunk],
        )

    def team_copy(out_box, in_box, send, recv, index, target, source):
        return pltpu.make_async_remote_copy(
            src_ref=out_box.at[index, target],
            dst_ref=in_box.at[index, source],
            send_sem=send.at[index, target],
            recv_sem=recv.at[index, source],
            device_id=place(base_team + target),
            device_id_type=MESH,
        )

    back_copy = functools.partial(team_copy, back_out, back_in, back_send, back_recv)

    def second_copy(tile, target, source):
        return pltpu.make_async_remote_copy(
            src_ref=second_out.at[tile, target],
            dst_ref=second_in.at[tile, source],
            send_sem=second_send.at[tile, target],
            recv_sem=second_recv.at[tile, source],
            device_id=place(target),
            device_id_type=MESH,
        )

    def last_copy(group, target, source):
        span = pl.ds(groups[group][0], groups[group][1] - groups[group][0])
        return pltpu.make_async_remote_copy(
            src_ref=last_out.at[target, span],
            dst_ref=last_in.at[source, span],
            send_sem=last_send.at[group, target],
            recv_sem=last_recv.at[group, source],
            device_id=place(target),
            device_id_type=MESH,
        )

    def back_own(tile):
        return pltpu.make_async_copy(
            back_out.at[tile, seat], back_in.at[tile, seat], own_sems.at[2, tile]
        )

    def second_own(tile):
        return pltpu.make_async_copy(
            second_out.at[tile, me], second_in.at[tile, me], own_sems.at[3, tile]
        )

    def last_own_copy(group):
        span = pl.ds(groups[group][0], groups[group][1] - groups[group][0])
        return pltpu.make_async_copy(
            last_out.at[me, span], last_in.at[me, span], last_own.at[group]
        )

    def far(step):
        return (me + step) % owners

    def near(step):
        return (seat + step) % team

    def send_left(chunk):
        left_own(chunk).start()
        each(1, team, lambda step: left_copy(chunk, near(step), seat).start())

    def send_right(chunk):
        def act(step):
            right_copy(chunk, other_team + near(step), me).start()
            right_copy(chunk, base_team + near(step), me).start()

        right_own(chunk).start()
        right_copy(chunk, other_team + seat, me).start()
        each(1, team, act)

    def project(update, flat):
        proj = lax.dot_general(
            proj_v[update], flat, (((1,), (1,)), ((), ())), preferred_element_type=jnp.float32
        )
        width = proj.shape[0] // 2
        return sigmoid(proj[width:]) * proj[:width]

    def mask_at(at):
        chunk, step = at // step_rows, at % step_rows
        return row * (2 * rows) + chunk * (2 * step_rows) + col * step_rows + step

    def produce_first(chunk):
        def one_row(step):
            at = chunk * step_rows + step
            token = mask_at(at)
            values = cells[at].reshape(tokens, channels).astype(jnp.float32)
            same = chain_v[...] == chain_s[token]
            start = (values + jnp.where(same, bias_v[...], 0.0)).astype(jnp.bfloat16)
            cells[at] = start.reshape(tiles, chips, pair_rows, channels)
            flat = normalise(start.astype(jnp.float32), 1)
            normed[at] = flat.reshape(tiles, lanes, channels)
            gated = (mask_s[token] * mask_v[...]) * project(0, flat)
            first_out[:, at] = gated.astype(jnp.bfloat16).reshape(team, 2 * per, tokens)

        each(0, step_rows, one_row)

    def widen(block, base):
        block = block.astype(jnp.float32).reshape(-1, block.shape[-1])
        size = block.shape[0]
        for tile in range(block.shape[1] // lanes):
            wide[tile, pl.ds(base, size), :] = block[:, tile * lanes : (tile + 1) * lanes]

    def pick(first, size, stride):
        pieces = [
            wide[tile, pl.ds(first, size, stride=stride), :].astype(jnp.bfloat16)
            for tile in range(tiles)
        ]
        return jnp.concatenate(pieces, axis=1)

    right_base = team_rows * per

    def widen_left(chunk, source):
        first = source * rows + chunk * step_rows
        widen(left_in[pl.ds(first, step_rows)], pl.multiple_of(first * per, per))

    def widen_right(chunk, source):
        first = source * step_rows
        base = pl.multiple_of(right_base + first * per, per)
        widen(right_in[chunk, pl.ds(first, step_rows)], base)

    def take_left():
        for chunk in range(CHUNKS):
            left_own(chunk).wait()
            widen_left(chunk, seat)

            def arrive(step):
                source = (seat + team - step) % team
                left_copy(chunk, seat, source).wait_recv()
                widen_left(chunk, source)

            each(1, team, arrive)

    def take_right(chunk):
        def arrive(step):
            source = (me + owners - step) % owners
            right_copy(chunk, me, source).wait_recv()
            widen_right(chunk, source)

        right_own(chunk).wait()
        widen_right(chunk, me)
        each(1, owners, arrive)

    def contract_first(tile):
        def channel(index):
            left = pick(index, team_rows, per)
            right = pick(right_base + index, lanes, per)
            tri = lax.dot_general(
                left, right, (((1,), (1,)), ((), ())), preferred_element_type=jnp.float32
            )
            products[pl.ds(index, team_rows, stride=per), :] = tri

        each(0, per, channel)
        size = rows * per

        def give(step):
            target = near(step)
            base = pl.multiple_of(target * size, size)
            back_out[tile, target] = products[pl.ds(base, size), :].astype(jnp.bfloat16)

            @pl.when(step > 0)
            def _():
                back_copy(tile, target, seat).start()

        each(0, team, give)
        back_own(tile).start()

    def finish(update, at, tile, tris):
        tri = jnp.concatenate(tris, axis=1)
        here = pl.ds(at, batch)
        change = lax.dot_general(
            normalise(tri, 0),
            outw_v[update],
            (((0,), (0,)), ((), ())),
            preferred_element_type=jnp.float32,
        )
        flat = normed[here, tile].reshape(batch * lanes, channels)
        gating = sigmoid(jnp.dot(flat, gate_v[update], preferred_element_type=jnp.float32))
        values = cells[here, tile].reshape(batch * lanes, channels).astype(jnp.float32)
        result = (values + gating * change).astype(jnp.bfloat16)
        cells[here, tile] = result.reshape(batch, chips, pair_rows, channels)
        return result

    def arrived(copy, index, people, own):
        each(1, people, lambda step: copy(index, own, (own + people - step) % people).wait_recv())

    def consume_first(tile):
        arrived(back_copy, tile, team, seat)
        back_own(tile).wait()
        mask_tile = mask_v[:, tile * lanes : (tile + 1) * lanes]

        def some_rows(step):
            at = step * batch
            tris = []
            for which in range(batch):
                base = pl.multiple_of((at + which) * per, per)
                tri = back_in[tile, :, pl.ds(base, per), :].astype(jnp.float32)
                tris.append(tri.reshape(team * per, lanes))
            result = finish(0, at, tile, tris)
            flat = normalise(result.astype(jnp.float32), 1)
            normed[pl.ds(at, batch), tile] = flat.reshape(batch, lanes, channels)
            gated = project(1, flat)
            for which in range(batch):
                mask = mask_s[mask_at(at + which)] * mask_tile
                piece = (mask * gated[:, which * lanes : (which + 1) * lanes]).astype(jnp.bfloat16)
                second_out[tile, :, at + which] = piece.reshape(owners, 2 * share, lanes)

        each(0, rows // batch, some_rows)
        second_own(tile).start()
        each(1, owners, lambda step: second_copy(tile, far(step), me).start())

    def take_second(tile):
        def put(source):
            size = rows * 2 * share
            block = second_in[tile, source].astype(jnp.float32).reshape(size, lanes)
            wide[tile, pl.ds(pl.multiple_of(source * size, size), size), :] = block

        def arrive(step):
            source = (me + owners - step) % owners
            second_copy(tile, me, source).wait_recv()
            put(source)

        second_own(tile).wait()
        put(me)
        each(1, owners, arrive)

    block_size = lanes * share

    def contract_second(newest):
        def channel(index):
            def side(tile, first):
                values = wide[tile, pl.ds(first, tokens, stride=2 * share), :]
                return values.astype(jnp.bfloat16)

            def product(left, right):
                return lax.dot_general(
                    left, right, (((0,), (0,)), ((), ())), preferred_element_type=jnp.float32
                )

            def store(chunk, tile, tri):
                first = blocks.index((chunk, tile)) * block_size
                products[pl.ds(first + index, lanes, stride=share), :] = tri

            lefts = [side(tile, index) for tile in range(newest + 1)]
            rights = [side(tile, share + index) for tile in range(newest + 1)]
            level = product(lefts[newest], jnp.concatenate(rights, axis=1))
            for tile in range(newest + 1):
                store(newest, tile, level[:, tile * lanes : (tile + 1) * lanes])
            if newest:
                upright = product(jnp.concatenate(lefts[:newest], axis=1), rights[newest])
                for chunk in range(newest):
                    store(chunk, newest, upright[chunk * lanes : (chunk + 1) * lanes])

        each(0, share, channel)
        size = step_rows * share
        for group, (first, last, when) in enumerate(groups):
            if when != newest:
                continue

            def give(step):
                target = far(step)
                for block in range(first, last):
                    base = pl.multiple_of(block * block_size + target * size, size)
                    last_out[target, block] = products[pl.ds(base, size), :].astype(jnp.bfloat16)

                @pl.when(step > 0)
                def _():
                    last_copy(group, target, me).start()

            each(0, owners, give)
            last_own_copy(group).start()

    def consume_second(group):
        arrived(last_copy, group, owners, me)
        last_own_copy(group).wait()
        for block in range(groups[group][0], groups[group][1]):
            chunk, tile = blocks[block]
            for first in range(0, step_rows, batch):
                tris = []
                for which in range(first, first + batch, 2):
                    two = last_in[:, block, which * share : (which + 2) * share, :]
                    two = two.astype(jnp.float32)
                    tris.append(two[:, :share].reshape(owners * share, lanes))
                    tris.append(two[:, share:].reshape(owners * share, lanes))
                finish(1, chunk * step_rows + first, tile, tris)
            for copy in out_copies(chunk, tile):
                copy.start()

    grid = [(chunk, tile) for chunk in range(CHUNKS) for tile in range(tiles)]
    for at in grid:
        for copy in pair_copies(*at):
            copy.start()
    for chunk in range(CHUNKS):
        for tile in range(tiles):
            for copy in pair_copies(chunk, tile):
                copy.wait()
        produce_first(chunk)
        if chunk == 0:
            send_right(0)
        send_left(chunk)
    for chunk in range(1, CHUNKS):
        send_right(chunk)
    take_left()
    for tile in range(tiles):
        take_right(tile)
        contract_first(tile)
        if tile:
            consume_first(tile - 1)
    consume_first(tiles - 1)
    for tile in range(tiles):
        take_second(tile)
        contract_second(tile)
    for group in range(len(groups)):
        consume_second(group)

    for chunk in range(CHUNKS):

        def sent(step):
            left_copy(chunk, near(step), seat).wait_send()
            right_copy(chunk, other_team + near(step), me).wait_send()
            right_copy(chunk, base_team + near(step), me).wait_send()
            back_copy(chunk, near(step), seat).wait_send()

        right_copy(chunk, other_team + seat, me).wait_send()
        each(1, team, sent)
    for tile in range(tiles):
        each(1, owners, lambda step: second_copy(tile, far(step), me).wait_send())
    for group in range(len(groups)):
        each(1, owners, lambda step: last_copy(group, far(step), me).wait_send())
    for at in grid:
        for copy in out_copies(*at):
            copy.wait()


def arrange(weight, groups):
    channels, width = weight.shape
    parts = weight.reshape(channels, 2, 2, groups, width // (4 * groups))
    return parts.transpose(2, 3, 1, 4, 0).reshape(width, channels)


def fused_shards(
    pair, chain_ids, token_mask, same_chain_bias, proj_weight, gate_weight, out_weight
):
    rows_tile, cols_tile, channels = pair.shape
    chips = lax.axis_size("row")
    owners = 2 * chips
    team = owners // 2
    tokens = 2 * cols_tile
    rows = rows_tile // 2
    step_rows = rows // CHUNKS
    hidden = proj_weight.shape[2] // 4
    per = hidden // team
    lanes = owners * step_rows
    share = hidden // owners
    blocks, groups = [len(part) for part in block_order()]
    proj = jnp.stack([arrange(proj_weight[0], team), arrange(proj_weight[1], owners)])

    def dealt(values):
        parts = values.reshape(chips, CHUNKS, 2 * step_rows)
        return parts.transpose(1, 0, 2).reshape(tokens)

    chain_cols = jnp.broadcast_to(dealt(chain_ids)[:, None], (tokens, channels))
    mask = token_mask.astype(jnp.float32)
    bf16, f32 = jnp.bfloat16, jnp.float32
    vmem = pl.BlockSpec(memory_space=pltpu.VMEM)
    smem = pl.BlockSpec(memory_space=pltpu.SMEM)
    anywhere = pl.BlockSpec(memory_space=pl.ANY)
    view = (rows_tile, chips // 2, CHUNKS, 2 * step_rows, channels)

    def sems(*shape):
        return pltpu.SemaphoreType.DMA(shape)

    result = pl.pallas_call(
        functools.partial(fused_kernel, chips),
        out_shape=jax.ShapeDtypeStruct(view, pair.dtype),
        in_specs=[anywhere, smem, smem, vmem, vmem, vmem, vmem, vmem, vmem],
        out_specs=anywhere,
        scratch_shapes=[
            pltpu.VMEM((rows, CHUNKS, chips, 2 * step_rows, channels), bf16),
            pltpu.VMEM((rows, CHUNKS, lanes, channels), bf16),
            pltpu.VMEM((team, rows, 2 * per, tokens), bf16),
            pltpu.VMEM((team * rows, per, tokens), bf16),
            pltpu.VMEM((CHUNKS, lanes, per, tokens), bf16),
            pltpu.VMEM((CHUNKS, team * rows * 2 * per, lanes), f32),
            pltpu.VMEM((blocks * lanes * share, lanes), f32),
            pltpu.VMEM((CHUNKS, team, rows * per, lanes), bf16),
            pltpu.VMEM((CHUNKS, team, rows * per, lanes), bf16),
            pltpu.VMEM((CHUNKS, owners, rows, 2 * share, lanes), bf16),
            pltpu.VMEM((CHUNKS, owners, rows, 2 * share, lanes), bf16),
            pltpu.VMEM((owners, blocks, step_rows * share, lanes), bf16),
            pltpu.VMEM((owners, blocks, step_rows * share, lanes), bf16),
            sems(3, CHUNKS, CHUNKS),
            sems(CHUNKS, team),
            sems(CHUNKS, team),
            sems(CHUNKS, owners),
            sems(CHUNKS, owners),
            sems(CHUNKS, team),
            sems(CHUNKS, team),
            sems(CHUNKS, owners),
            sems(CHUNKS, owners),
            sems(groups, owners),
            sems(groups, owners),
            sems(4, CHUNKS),
            sems(groups),
            sems(3, CHUNKS, CHUNKS),
        ],
        compiler_params=pltpu.CompilerParams(
            collective_id=0, has_side_effects=True, vmem_limit_bytes=60 * 1024 * 1024
        ),
    )(
        pair.reshape(view),
        chain_ids,
        mask,
        chain_cols,
        dealt(mask)[None, :],
        same_chain_bias.astype(f32)[None, :],
        proj,
        gate_weight,
        out_weight,
    )
    return result.reshape(pair.shape)


def fits(pair, proj_weight):
    rows_tile, cols_tile, channels = pair.shape
    rows_grid, cols_grid = lax.axis_size("row"), lax.axis_size("col")
    hidden = proj_weight.shape[2] // 4
    return (
        cols_grid == 2
        and rows_grid % 2 == 0
        and hidden == 8 * cols_grid * rows_grid
        and channels == 128
        and rows_tile % (4 * CHUNKS) == 0
        and cols_tile % 64 == 0
        and rows_tile * rows_grid == 128 * CHUNKS
        and rows_tile * rows_grid == cols_tile * cols_grid
    )


def program_shards(pair, chain_ids, token_mask, same_chain_bias, proj_weight, *rest):
    chosen = fused_shards if fits(pair, proj_weight) else shards
    return chosen(pair, chain_ids, token_mask, same_chain_bias, proj_weight, *rest)


def solution(mesh):
    return jax.shard_map(
        program_shards,
        mesh=mesh,
        in_specs=(P(("group", "row"), "col", None), P("group"), P("group"), P(), P(), P(), P()),
        out_specs=P(("group", "row"), "col", None),
        check_vma=False,
    )
```

```python
import functools

import jax
import jax.numpy as jnp
from jax import lax
from jax.experimental import pallas as pl
from jax.experimental.pallas import tpu as pltpu
from jax.sharding import PartitionSpec as P

MESH = pl.DeviceIdType.MESH
CHUNKS = 3


def layer_norm(values):
    mean = jnp.mean(values, axis=-1, keepdims=True)
    centred = values - mean
    var = jnp.mean(centred * centred, axis=-1, keepdims=True)
    return centred * lax.rsqrt(var + 1e-05)


def make_contract(rows_grid, cols_grid, rows_tile, cols_tile, incoming):

    def contract(pieces):
        items = pieces.shape[2]
        total = rows_grid * rows_tile
        whole = pieces.reshape(rows_grid, cols_grid, 2, items, rows_tile, cols_tile)
        whole = whole.transpose(2, 3, 0, 4, 1, 5).reshape(2, items, total, cols_grid * cols_tile)
        if incoming:
            tri = jnp.einsum("mki,mkj->mij", whole[0], whole[1], preferred_element_type=jnp.float32)
        else:
            tri = jnp.einsum("mik,mjk->mij", whole[0], whole[1], preferred_element_type=jnp.float32)
        tri = tri.astype(jnp.bfloat16)
        tri = tri.reshape(items, rows_grid, rows_tile, cols_grid, cols_tile).transpose(
            1, 3, 0, 2, 4
        )
        return tri.reshape(rows_grid * cols_grid, items, rows_tile * cols_tile)

    return contract


def triangle(pair_now, mask_flat, proj, gate, outw, incoming):
    rows_tile, cols_tile, channels = pair_now.shape
    hidden = proj.shape[1] // 4
    rows_grid = lax.axis_size("row")
    cols_grid = lax.axis_size("col")
    owners = rows_grid * cols_grid
    per_owner = hidden // owners
    cells = rows_tile * cols_tile
    normed = layer_norm(pair_now.astype(jnp.float32)).astype(jnp.bfloat16).reshape(cells, channels)
    proj_out = jnp.dot(normed, proj, preferred_element_type=jnp.float32)
    left = (
        mask_flat * jax.nn.sigmoid(proj_out[:, hidden : 2 * hidden]) * proj_out[:, 0:hidden]
    ).astype(jnp.bfloat16)
    right = (
        mask_flat
        * jax.nn.sigmoid(proj_out[:, 3 * hidden : 4 * hidden])
        * proj_out[:, 2 * hidden : 3 * hidden]
    ).astype(jnp.bfloat16)
    stacked = jnp.stack([left, right]).reshape(2, cells, owners, per_owner).transpose(2, 0, 3, 1)
    contract = make_contract(rows_grid, cols_grid, rows_tile, cols_tile, incoming)
    result = contract(
        lax.all_to_all(stacked, ("row", "col"), split_axis=0, concat_axis=0, tiled=True)
    )
    returned = lax.all_to_all(result, ("row", "col"), split_axis=0, concat_axis=0, tiled=True)
    tri = returned.reshape(hidden, cells).T
    normed_tri = layer_norm(tri.astype(jnp.float32)).astype(jnp.bfloat16)
    update = jnp.dot(normed_tri, outw, preferred_element_type=jnp.float32)
    gating = jax.nn.sigmoid(jnp.dot(normed, gate, preferred_element_type=jnp.float32))
    result_flat = pair_now.reshape(cells, channels).astype(jnp.float32) + gating * update
    return result_flat.astype(jnp.bfloat16).reshape(rows_tile, cols_tile, channels)


def shards(pair, chain_ids, token_mask, same_chain_bias, proj_weight, gate_weight, out_weight):
    rows_tile, cols_tile, channels = pair.shape
    row_index = lax.axis_index("row")
    col_index = lax.axis_index("col")
    row_start = row_index * rows_tile
    col_start = col_index * cols_tile
    chain_rows = lax.dynamic_slice_in_dim(chain_ids, row_start, rows_tile)
    chain_cols = lax.dynamic_slice_in_dim(chain_ids, col_start, cols_tile)
    mask_rows = lax.dynamic_slice_in_dim(token_mask, row_start, rows_tile).astype(jnp.float32)
    mask_cols = lax.dynamic_slice_in_dim(token_mask, col_start, cols_tile).astype(jnp.float32)
    same = (chain_rows[:, None] == chain_cols[None, :]).astype(jnp.float32)
    start = (
        pair.astype(jnp.float32)
        + same[:, :, None] * same_chain_bias.astype(jnp.float32)[None, None, :]
    ).astype(jnp.bfloat16)
    mask_flat = (mask_rows[:, None] * mask_cols[None, :]).reshape(rows_tile * cols_tile, 1)
    first = triangle(start, mask_flat, proj_weight[0], gate_weight[0], out_weight[0], False)
    return triangle(first, mask_flat, proj_weight[1], gate_weight[1], out_weight[1], True)


def sigmoid(values):
    return 0.5 * jnp.tanh(0.5 * values) + 0.5


def normalise(values, axis):
    mean = jnp.mean(values, axis=axis, keepdims=True)
    centred = values - mean
    var = jnp.mean(centred * centred, axis=axis, keepdims=True)
    return (centred * lax.rsqrt(var + 1e-05)).astype(jnp.bfloat16)


def block_order():
    blocks, groups = [], []
    for newest in range(CHUNKS):
        first = len(blocks)
        for older in range(newest):
            blocks += [(older, newest), (newest, older)]
        blocks.append((newest, newest))
        cut = first + (len(blocks) - first) // 2 if newest == CHUNKS - 1 else len(blocks)
        groups.append((first, cut, newest))
        if cut < len(blocks):
            groups.append((cut, len(blocks), newest))
    return blocks, groups


def fused_kernel(
    rows_grid,
    pair_ref,
    chain_s,
    mask_s,
    chain_v,
    mask_v,
    bias_v,
    proj_v,
    gate_v,
    outw_v,
    out_ref,
    turned,
    cells,
    normed,
    first_out,
    left_in,
    right_in,
    wide,
    products,
    back_out,
    back_in,
    second_out,
    second_in,
    last_out,
    last_in,
    pair_sems,
    left_send,
    left_recv,
    right_send,
    right_recv,
    back_send,
    back_recv,
    second_send,
    second_recv,
    last_send,
    last_recv,
    own_sems,
    last_own,
    out_sems,
):
    owners = 2 * rows_grid
    team = owners // 2
    rows, tiles, chips, pair_rows, channels = cells.shape
    step_rows = rows // CHUNKS
    lanes = chips * pair_rows
    tokens = tiles * lanes
    per = left_in.shape[1]
    team_rows = team * rows
    batch = 4
    row, col = lax.axis_index("row"), lax.axis_index("col")
    me = row * 2 + col
    seat = me % team
    base_team = me - seat
    other_team = team - base_team
    sibling = {"row": row, "col": 1 - col}
    half_chips = chips // 2
    share = team * per // owners
    blocks, groups = block_order()

    def place(owner):
        return {"row": owner // 2, "col": owner % 2}

    def each(first, last, act):
        def body(step, carry):
            act(step)
            return carry

        lax.fori_loop(first, last, body, 0)

    barrier = pltpu.get_barrier_semaphore()

    def greet(step):
        pl.semaphore_signal(
            barrier, inc=1, device_id=place((me + step) % owners), device_id_type=MESH
        )

    each(1, owners, greet)
    pl.semaphore_wait(barrier, owners - 1)

    def part(chunk):
        return pl.ds(chunk * step_rows, step_rows)

    def tile_rows(chunk, core):
        return pl.ds(chunk * (2 * step_rows) + core * step_rows, step_rows)

    def pair_copies(chunk, tile):
        into = cells.at[part(chunk), tile, pl.ds(col * half_chips, half_chips)]
        own = pltpu.make_async_copy(
            pair_ref.at[tile_rows(chunk, col), :, tile], into, pair_sems.at[0, chunk, tile]
        )
        other = pltpu.make_async_remote_copy(
            src_ref=pair_ref.at[tile_rows(chunk, 1 - col), :, tile],
            dst_ref=into,
            send_sem=pair_sems.at[1, chunk, tile],
            recv_sem=pair_sems.at[2, chunk, tile],
            device_id=sibling,
            device_id_type=MESH,
        )
        return own, other

    def out_copies(chunk, tile):
        to = out_ref.at[tile_rows(chunk, col), :, tile]
        own = pltpu.make_async_copy(
            cells.at[part(chunk), tile, pl.ds(col * half_chips, half_chips)],
            to,
            out_sems.at[0, chunk, tile],
        )
        other = pltpu.make_async_remote_copy(
            src_ref=cells.at[part(chunk), tile, pl.ds((1 - col) * half_chips, half_chips)],
            dst_ref=to,
            send_sem=out_sems.at[1, chunk, tile],
            recv_sem=out_sems.at[2, chunk, tile],
            device_id=sibling,
            device_id_type=MESH,
        )
        return own, other

    def left_copy(chunk, target, source):
        return pltpu.make_async_remote_copy(
            src_ref=first_out.at[target, part(chunk), pl.ds(0, per)],
            dst_ref=left_in.at[pl.ds(source * rows + chunk * step_rows, step_rows)],
            send_sem=left_send.at[chunk, target],
            recv_sem=left_recv.at[chunk, source],
            device_id=place(base_team + target),
            device_id_type=MESH,
        )

    def left_own(chunk):
        return pltpu.make_async_copy(
            first_out.at[seat, part(chunk), pl.ds(0, per)],
            left_in.at[pl.ds(seat * rows + chunk * step_rows, step_rows)],
            own_sems.at[0, chunk],
        )

    def right_copy(chunk, target, source):
        return pltpu.make_async_remote_copy(
            src_ref=first_out.at[target % team, part(chunk), pl.ds(per, per)],
            dst_ref=right_in.at[chunk, pl.ds(source * step_rows, step_rows)],
            send_sem=right_send.at[chunk, target],
            recv_sem=right_recv.at[chunk, source],
            device_id=place(target),
            device_id_type=MESH,
        )

    def right_own(chunk):
        return pltpu.make_async_copy(
            first_out.at[seat, part(chunk), pl.ds(per, per)],
            right_in.at[chunk, pl.ds(me * step_rows, step_rows)],
            own_sems.at[1, chunk],
        )

    def team_copy(out_box, in_box, send, recv, index, target, source):
        return pltpu.make_async_remote_copy(
            src_ref=out_box.at[index, target],
            dst_ref=in_box.at[index, source],
            send_sem=send.at[index, target],
            recv_sem=recv.at[index, source],
            device_id=place(base_team + target),
            device_id_type=MESH,
        )

    back_copy = functools.partial(team_copy, back_out, back_in, back_send, back_recv)

    def second_copy(tile, target, source):
        return pltpu.make_async_remote_copy(
            src_ref=second_out.at[tile, target],
            dst_ref=second_in.at[tile, source],
            send_sem=second_send.at[tile, target],
            recv_sem=second_recv.at[tile, source],
            device_id=place(target),
            device_id_type=MESH,
        )

    def last_copy(group, target, source):
        span = pl.ds(groups[group][0], groups[group][1] - groups[group][0])
        return pltpu.make_async_remote_copy(
            src_ref=last_out.at[target, span],
            dst_ref=last_in.at[source, span],
            send_sem=last_send.at[group, target],
            recv_sem=last_recv.at[group, source],
            device_id=place(target),
            device_id_type=MESH,
        )

    def back_own(tile):
        return pltpu.make_async_copy(
            back_out.at[tile, seat], back_in.at[tile, seat], own_sems.at[2, tile]
        )

    def second_own(tile):
        return pltpu.make_async_copy(
            second_out.at[tile, me], second_in.at[tile, me], own_sems.at[3, tile]
        )

    def last_own_copy(group):
        span = pl.ds(groups[group][0], groups[group][1] - groups[group][0])
        return pltpu.make_async_copy(
            last_out.at[me, span], last_in.at[me, span], last_own.at[group]
        )

    def far(step):
        return (me + step) % owners

    def near(step):
        return (seat + step) % team

    def send_left(chunk):
        left_own(chunk).start()
        each(1, team, lambda step: left_copy(chunk, near(step), seat).start())

    def send_right(chunk):
        def act(step):
            right_copy(chunk, other_team + near(step), me).start()
            right_copy(chunk, base_team + near(step), me).start()

        right_own(chunk).start()
        right_copy(chunk, other_team + seat, me).start()
        each(1, team, act)

    def project(update, flat):
        proj = lax.dot_general(
            turned[update], flat, (((1,), (1,)), ((), ())), preferred_element_type=jnp.float32
        )
        width = proj.shape[0] // 4
        left = sigmoid(proj[width : 2 * width]) * proj[:width]
        right = sigmoid(proj[3 * width :]) * proj[2 * width : 3 * width]
        return left, right

    def mask_at(at):
        chunk, step = at // step_rows, at % step_rows
        return row * (2 * rows) + chunk * (2 * step_rows) + col * step_rows + step

    def produce_first(chunk):
        bias = bias_v[...].astype(jnp.float32)

        def one_row(step):
            at = chunk * step_rows + step
            token = mask_at(at)
            values = cells[at].reshape(tokens, channels).astype(jnp.float32)
            same = chain_v[...] == chain_s[token]
            start = (values + jnp.where(same, bias, 0.0)).astype(jnp.bfloat16)
            cells[at] = start.reshape(tiles, chips, pair_rows, channels)
            flat = normalise(start.astype(jnp.float32), 1)
            normed[at] = flat.reshape(tiles, lanes, channels)
            mask = mask_s[token].astype(jnp.float32) * mask_v[...]
            for side, gated in enumerate(project(0, flat)):
                piece = (mask * gated).astype(jnp.bfloat16).reshape(team, per, tokens)
                first_out[:, at, side * per : (side + 1) * per] = piece

        each(0, step_rows, one_row)

    def widen(block, base):
        block = block.astype(jnp.float32).reshape(-1, block.shape[-1])
        size = block.shape[0]
        for tile in range(block.shape[1] // lanes):
            wide[tile, pl.ds(base, size), :] = block[:, tile * lanes : (tile + 1) * lanes]

    def pick(first, size, stride):
        pieces = [
            wide[tile, pl.ds(first, size, stride=stride), :].astype(jnp.bfloat16)
            for tile in range(tiles)
        ]
        return jnp.concatenate(pieces, axis=1)

    right_base = team_rows * per

    def widen_left(chunk, source):
        first = source * rows + chunk * step_rows
        widen(left_in[pl.ds(first, step_rows)], pl.multiple_of(first * per, per))

    def widen_right(chunk, source):
        first = source * step_rows
        base = pl.multiple_of(right_base + first * per, per)
        widen(right_in[chunk, pl.ds(first, step_rows)], base)

    def take_left():
        for chunk in range(CHUNKS):
            left_own(chunk).wait()
            widen_left(chunk, seat)

            def arrive(step):
                source = (seat + team - step) % team
                left_copy(chunk, seat, source).wait_recv()
                widen_left(chunk, source)

            each(1, team, arrive)

    def take_right(chunk):
        def arrive(step):
            source = (me + owners - step) % owners
            right_copy(chunk, me, source).wait_recv()
            widen_right(chunk, source)

        right_own(chunk).wait()
        widen_right(chunk, me)
        each(1, owners, arrive)

    def contract_first(tile):
        def channel(index):
            left = pick(index, team_rows, per)
            right = pick(right_base + index, lanes, per)
            tri = lax.dot_general(
                left, right, (((1,), (1,)), ((), ())), preferred_element_type=jnp.float32
            )
            products[pl.ds(index, team_rows, stride=per), :] = tri

        each(0, per, channel)
        size = rows * per

        def give(step):
            target = near(step)
            base = pl.multiple_of(target * size, size)
            back_out[tile, target] = products[pl.ds(base, size), :].astype(jnp.bfloat16)

            @pl.when(step > 0)
            def _():
                back_copy(tile, target, seat).start()

        each(0, team, give)
        back_own(tile).start()

    def finish(update, at, tile, tris):
        tri = jnp.concatenate(tris, axis=1)
        here = pl.ds(at, batch)
        change = lax.dot_general(
            normalise(tri, 0),
            outw_v[update],
            (((0,), (0,)), ((), ())),
            preferred_element_type=jnp.float32,
        )
        flat = normed[here, tile].reshape(batch * lanes, channels)
        gating = sigmoid(jnp.dot(flat, gate_v[update], preferred_element_type=jnp.float32))
        values = cells[here, tile].reshape(batch * lanes, channels).astype(jnp.float32)
        result = (values + gating * change).astype(jnp.bfloat16)
        cells[here, tile] = result.reshape(batch, chips, pair_rows, channels)
        return result

    def arrived(copy, index, people, own):
        each(1, people, lambda step: copy(index, own, (own + people - step) % people).wait_recv())

    def consume_first(tile):
        arrived(back_copy, tile, team, seat)
        back_own(tile).wait()
        mask_tile = mask_v[:, tile * lanes : (tile + 1) * lanes]

        def some_rows(step):
            at = step * batch
            tris = []
            for which in range(batch):
                base = pl.multiple_of((at + which) * per, per)
                tri = back_in[tile, :, pl.ds(base, per), :].astype(jnp.float32)
                tris.append(tri.reshape(team * per, lanes))
            result = finish(0, at, tile, tris)
            flat = normalise(result.astype(jnp.float32), 1)
            normed[pl.ds(at, batch), tile] = flat.reshape(batch, lanes, channels)
            left, right = project(1, flat)
            for which in range(batch):
                mask = mask_s[mask_at(at + which)].astype(jnp.float32) * mask_tile
                span = slice(which * lanes, (which + 1) * lanes)
                pieces = [
                    (mask * gated[:, span]).reshape(owners, share, lanes)
                    for gated in (left, right)
                ]
                piece = jnp.concatenate(pieces, axis=1).astype(jnp.bfloat16)
                second_out[tile, :, at + which] = piece

        each(0, rows // batch, some_rows)
        second_own(tile).start()
        each(1, owners, lambda step: second_copy(tile, far(step), me).start())

    def take_second(tile):
        def put(source):
            size = rows * 2 * share
            block = second_in[tile, source].astype(jnp.float32).reshape(size, lanes)
            wide[tile, pl.ds(pl.multiple_of(source * size, size), size), :] = block

        def arrive(step):
            source = (me + owners - step) % owners
            second_copy(tile, me, source).wait_recv()
            put(source)

        second_own(tile).wait()
        put(me)
        each(1, owners, arrive)

    block_size = lanes * share

    def contract_second(newest):
        def channel(index):
            def side(tile, first):
                values = wide[tile, pl.ds(first, tokens, stride=2 * share), :]
                return values.astype(jnp.bfloat16)

            def product(left, right):
                return lax.dot_general(
                    left, right, (((0,), (0,)), ((), ())), preferred_element_type=jnp.float32
                )

            def store(chunk, tile, tri):
                first = blocks.index((chunk, tile)) * block_size
                products[pl.ds(first + index, lanes, stride=share), :] = tri

            lefts = [side(tile, index) for tile in range(newest + 1)]
            rights = [side(tile, share + index) for tile in range(newest + 1)]
            level = product(lefts[newest], jnp.concatenate(rights, axis=1))
            for tile in range(newest + 1):
                store(newest, tile, level[:, tile * lanes : (tile + 1) * lanes])
            if newest:
                upright = product(jnp.concatenate(lefts[:newest], axis=1), rights[newest])
                for chunk in range(newest):
                    store(chunk, newest, upright[chunk * lanes : (chunk + 1) * lanes])

        each(0, share, channel)
        size = step_rows * share
        for group, (first, last, when) in enumerate(groups):
            if when != newest:
                continue

            def give(step):
                target = far(step)
                for block in range(first, last):
                    base = pl.multiple_of(block * block_size + target * size, size)
                    last_out[target, block] = products[pl.ds(base, size), :].astype(jnp.bfloat16)

                @pl.when(step > 0)
                def _():
                    last_copy(group, target, me).start()

            each(0, owners, give)
            last_own_copy(group).start()

    def consume_second(group):
        arrived(last_copy, group, owners, me)
        last_own_copy(group).wait()
        for block in range(groups[group][0], groups[group][1]):
            chunk, tile = blocks[block]
            for first in range(0, step_rows, batch):
                tris = []
                for which in range(first, first + batch, 2):
                    two = last_in[:, block, which * share : (which + 2) * share, :]
                    two = two.astype(jnp.float32)
                    tris.append(two[:, :share].reshape(owners * share, lanes))
                    tris.append(two[:, share:].reshape(owners * share, lanes))
                finish(1, chunk * step_rows + first, tile, tris)
            for copy in out_copies(chunk, tile):
                copy.start()

    grid = [(chunk, tile) for chunk in range(CHUNKS) for tile in range(tiles)]
    for at in grid:
        for copy in pair_copies(*at):
            copy.start()
    for update in range(2):
        turned[update] = proj_v[update].astype(jnp.float32).T.astype(jnp.bfloat16)
    for chunk in range(CHUNKS):
        for tile in range(tiles):
            for copy in pair_copies(chunk, tile):
                copy.wait()
        produce_first(chunk)
        if chunk == 0:
            send_right(0)
        send_left(chunk)
    for chunk in range(1, CHUNKS):
        send_right(chunk)
    take_left()
    for tile in range(tiles):
        take_right(tile)
        contract_first(tile)
        if tile:
            consume_first(tile - 1)
    consume_first(tiles - 1)
    for tile in range(tiles):
        take_second(tile)
        contract_second(tile)
    for group in range(len(groups)):
        consume_second(group)

    for chunk in range(CHUNKS):

        def sent(step):
            left_copy(chunk, near(step), seat).wait_send()
            right_copy(chunk, other_team + near(step), me).wait_send()
            right_copy(chunk, base_team + near(step), me).wait_send()
            back_copy(chunk, near(step), seat).wait_send()

        right_copy(chunk, other_team + seat, me).wait_send()
        each(1, team, sent)
    for tile in range(tiles):
        each(1, owners, lambda step: second_copy(tile, far(step), me).wait_send())
    for group in range(len(groups)):
        each(1, owners, lambda step: last_copy(group, far(step), me).wait_send())
    for at in grid:
        for copy in out_copies(*at):
            copy.wait()


def fused_shards(
    pair, chain_ids, token_mask, same_chain_bias, proj_weight, gate_weight, out_weight
):
    rows_tile, cols_tile, channels = pair.shape
    chips = lax.axis_size("row")
    owners = 2 * chips
    team = owners // 2
    tokens = 2 * cols_tile
    rows = rows_tile // 2
    step_rows = rows // CHUNKS
    hidden = proj_weight.shape[2] // 4
    per = hidden // team
    lanes = owners * step_rows
    share = hidden // owners
    blocks, groups = [len(part) for part in block_order()]

    def dealt(values):
        parts = values.reshape(chips, CHUNKS, 2 * step_rows)
        return parts.transpose(1, 0, 2).reshape(tokens)

    chain_cols = jnp.broadcast_to(dealt(chain_ids)[:, None], (tokens, channels))
    bf16, f32 = jnp.bfloat16, jnp.float32
    vmem = pl.BlockSpec(memory_space=pltpu.VMEM)
    smem = pl.BlockSpec(memory_space=pltpu.SMEM)
    anywhere = pl.BlockSpec(memory_space=pl.ANY)
    view = (rows_tile, chips // 2, CHUNKS, 2 * step_rows, channels)

    def sems(*shape):
        return pltpu.SemaphoreType.DMA(shape)

    result = pl.pallas_call(
        functools.partial(fused_kernel, chips),
        out_shape=jax.ShapeDtypeStruct(view, pair.dtype),
        in_specs=[anywhere, smem, smem, vmem, vmem, vmem, vmem, vmem, vmem],
        out_specs=anywhere,
        scratch_shapes=[
            pltpu.VMEM((2, 4 * hidden, channels), bf16),
            pltpu.VMEM((rows, CHUNKS, chips, 2 * step_rows, channels), bf16),
            pltpu.VMEM((rows, CHUNKS, lanes, channels), bf16),
            pltpu.VMEM((team, rows, 2 * per, tokens), bf16),
            pltpu.VMEM((team * rows, per, tokens), bf16),
            pltpu.VMEM((CHUNKS, lanes, per, tokens), bf16),
            pltpu.VMEM((CHUNKS, team * rows * 2 * per, lanes), f32),
            pltpu.VMEM((blocks * lanes * share, lanes), f32),
            pltpu.VMEM((CHUNKS, team, rows * per, lanes), bf16),
            pltpu.VMEM((CHUNKS, team, rows * per, lanes), bf16),
            pltpu.VMEM((CHUNKS, owners, rows, 2 * share, lanes), bf16),
            pltpu.VMEM((CHUNKS, owners, rows, 2 * share, lanes), bf16),
            pltpu.VMEM((owners, blocks, step_rows * share, lanes), bf16),
            pltpu.VMEM((owners, blocks, step_rows * share, lanes), bf16),
            sems(3, CHUNKS, CHUNKS),
            sems(CHUNKS, team),
            sems(CHUNKS, team),
            sems(CHUNKS, owners),
            sems(CHUNKS, owners),
            sems(CHUNKS, team),
            sems(CHUNKS, team),
            sems(CHUNKS, owners),
            sems(CHUNKS, owners),
            sems(groups, owners),
            sems(groups, owners),
            sems(4, CHUNKS),
            sems(groups),
            sems(3, CHUNKS, CHUNKS),
        ],
        compiler_params=pltpu.CompilerParams(
            collective_id=0, has_side_effects=True, vmem_limit_bytes=60 * 1024 * 1024
        ),
    )(
        pair.reshape(view),
        chain_ids,
        token_mask,
        chain_cols,
        dealt(token_mask).astype(f32)[None, :],
        same_chain_bias[None, :],
        proj_weight,
        gate_weight,
        out_weight,
    )
    return result.reshape(pair.shape)


def fits(pair, proj_weight):
    rows_tile, cols_tile, channels = pair.shape
    rows_grid, cols_grid = lax.axis_size("row"), lax.axis_size("col")
    hidden = proj_weight.shape[2] // 4
    return (
        cols_grid == 2
        and rows_grid % 2 == 0
        and hidden == 8 * cols_grid * rows_grid
        and channels == 128
        and rows_tile % (4 * CHUNKS) == 0
        and cols_tile % 64 == 0
        and rows_tile * rows_grid == 128 * CHUNKS
        and rows_tile * rows_grid == cols_tile * cols_grid
    )


def program_shards(pair, chain_ids, token_mask, same_chain_bias, proj_weight, *rest):
    chosen = fused_shards if fits(pair, proj_weight) else shards
    return chosen(pair, chain_ids, token_mask, same_chain_bias, proj_weight, *rest)


def solution(mesh):
    return jax.shard_map(
        program_shards,
        mesh=mesh,
        in_specs=(P(("group", "row"), "col", None), P("group"), P("group"), P(), P(), P(), P()),
        out_specs=P(("group", "row"), "col", None),
        check_vma=False,
    )
```

```python
import functools

import jax
import jax.numpy as jnp
from jax import lax
from jax.experimental import pallas as pl
from jax.experimental.pallas import tpu as pltpu
from jax.sharding import PartitionSpec as P

MESH = pl.DeviceIdType.MESH
CHUNKS = 3


def layer_norm(values):
    mean = jnp.mean(values, axis=-1, keepdims=True)
    centred = values - mean
    var = jnp.mean(centred * centred, axis=-1, keepdims=True)
    return centred * lax.rsqrt(var + 1e-05)


def make_contract(rows_grid, cols_grid, rows_tile, cols_tile, incoming):

    def contract(pieces):
        items = pieces.shape[2]
        total = rows_grid * rows_tile
        whole = pieces.reshape(rows_grid, cols_grid, 2, items, rows_tile, cols_tile)
        whole = whole.transpose(2, 3, 0, 4, 1, 5).reshape(2, items, total, cols_grid * cols_tile)
        if incoming:
            tri = jnp.einsum("mki,mkj->mij", whole[0], whole[1], preferred_element_type=jnp.float32)
        else:
            tri = jnp.einsum("mik,mjk->mij", whole[0], whole[1], preferred_element_type=jnp.float32)
        tri = tri.astype(jnp.bfloat16)
        tri = tri.reshape(items, rows_grid, rows_tile, cols_grid, cols_tile).transpose(
            1, 3, 0, 2, 4
        )
        return tri.reshape(rows_grid * cols_grid, items, rows_tile * cols_tile)

    return contract


def triangle(pair_now, mask_flat, proj, gate, outw, incoming):
    rows_tile, cols_tile, channels = pair_now.shape
    hidden = proj.shape[1] // 4
    rows_grid = lax.axis_size("row")
    cols_grid = lax.axis_size("col")
    owners = rows_grid * cols_grid
    per_owner = hidden // owners
    cells = rows_tile * cols_tile
    normed = layer_norm(pair_now.astype(jnp.float32)).astype(jnp.bfloat16).reshape(cells, channels)
    proj_out = jnp.dot(normed, proj, preferred_element_type=jnp.float32)
    left = (
        mask_flat * jax.nn.sigmoid(proj_out[:, hidden : 2 * hidden]) * proj_out[:, 0:hidden]
    ).astype(jnp.bfloat16)
    right = (
        mask_flat
        * jax.nn.sigmoid(proj_out[:, 3 * hidden : 4 * hidden])
        * proj_out[:, 2 * hidden : 3 * hidden]
    ).astype(jnp.bfloat16)
    stacked = jnp.stack([left, right]).reshape(2, cells, owners, per_owner).transpose(2, 0, 3, 1)
    contract = make_contract(rows_grid, cols_grid, rows_tile, cols_tile, incoming)
    result = contract(
        lax.all_to_all(stacked, ("row", "col"), split_axis=0, concat_axis=0, tiled=True)
    )
    returned = lax.all_to_all(result, ("row", "col"), split_axis=0, concat_axis=0, tiled=True)
    tri = returned.reshape(hidden, cells).T
    normed_tri = layer_norm(tri.astype(jnp.float32)).astype(jnp.bfloat16)
    update = jnp.dot(normed_tri, outw, preferred_element_type=jnp.float32)
    gating = jax.nn.sigmoid(jnp.dot(normed, gate, preferred_element_type=jnp.float32))
    result_flat = pair_now.reshape(cells, channels).astype(jnp.float32) + gating * update
    return result_flat.astype(jnp.bfloat16).reshape(rows_tile, cols_tile, channels)


def shards(pair, chain_ids, token_mask, same_chain_bias, proj_weight, gate_weight, out_weight):
    rows_tile, cols_tile, channels = pair.shape
    row_index = lax.axis_index("row")
    col_index = lax.axis_index("col")
    row_start = row_index * rows_tile
    col_start = col_index * cols_tile
    chain_rows = lax.dynamic_slice_in_dim(chain_ids, row_start, rows_tile)
    chain_cols = lax.dynamic_slice_in_dim(chain_ids, col_start, cols_tile)
    mask_rows = lax.dynamic_slice_in_dim(token_mask, row_start, rows_tile).astype(jnp.float32)
    mask_cols = lax.dynamic_slice_in_dim(token_mask, col_start, cols_tile).astype(jnp.float32)
    same = (chain_rows[:, None] == chain_cols[None, :]).astype(jnp.float32)
    start = (
        pair.astype(jnp.float32)
        + same[:, :, None] * same_chain_bias.astype(jnp.float32)[None, None, :]
    ).astype(jnp.bfloat16)
    mask_flat = (mask_rows[:, None] * mask_cols[None, :]).reshape(rows_tile * cols_tile, 1)
    first = triangle(start, mask_flat, proj_weight[0], gate_weight[0], out_weight[0], False)
    return triangle(first, mask_flat, proj_weight[1], gate_weight[1], out_weight[1], True)


def sigmoid(values):
    return 0.5 * jnp.tanh(0.5 * values) + 0.5


def normalise(values, axis):
    mean = jnp.mean(values, axis=axis, keepdims=True)
    centred = values - mean
    var = jnp.mean(centred * centred, axis=axis, keepdims=True)
    return (centred * lax.rsqrt(var + 1e-05)).astype(jnp.bfloat16)


def block_order():
    blocks, groups = [], []
    for newest in range(CHUNKS):
        first = len(blocks)
        for older in range(newest):
            blocks += [(older, newest), (newest, older)]
        blocks.append((newest, newest))
        run = 2 if newest == CHUNKS - 1 else len(blocks)
        for start in range(first, len(blocks), run):
            groups.append((start, min(start + run, len(blocks)), newest))
    return blocks, groups


def fused_kernel(
    rows_grid,
    pair_ref,
    chain_s,
    mask_s,
    chain_v,
    mask_v,
    bias_v,
    proj_v,
    gate_v,
    outw_v,
    out_ref,
    turned,
    cells,
    normed,
    first_out,
    left_in,
    right_in,
    wide,
    products,
    back_out,
    back_in,
    second_out,
    second_in,
    last_out,
    last_in,
    pair_sems,
    left_send,
    left_recv,
    right_send,
    right_recv,
    back_send,
    back_recv,
    second_send,
    second_recv,
    last_send,
    last_recv,
    own_sems,
    last_own,
    out_sems,
):
    owners = 2 * rows_grid
    team = owners // 2
    rows, tiles, chips, pair_rows, channels = cells.shape
    step_rows = rows // CHUNKS
    lanes = chips * pair_rows
    tokens = tiles * lanes
    per = left_in.shape[1]
    team_rows = team * rows
    batch = 4
    row, col = lax.axis_index("row"), lax.axis_index("col")
    me = row * 2 + col
    seat = me % team
    base_team = me - seat
    other_team = team - base_team
    sibling = {"row": row, "col": 1 - col}
    half_chips = chips // 2
    share = team * per // owners
    blocks, groups = block_order()

    def place(owner):
        return {"row": owner // 2, "col": owner % 2}

    def each(first, last, act):
        def body(step, carry):
            act(step)
            return carry

        lax.fori_loop(first, last, body, 0)

    barrier = pltpu.get_barrier_semaphore()

    def greet(step):
        pl.semaphore_signal(
            barrier, inc=1, device_id=place((me + step) % owners), device_id_type=MESH
        )

    each(1, owners, greet)
    pl.semaphore_wait(barrier, owners - 1)

    def part(chunk):
        return pl.ds(chunk * step_rows, step_rows)

    def tile_rows(chunk, core):
        return pl.ds(chunk * (2 * step_rows) + core * step_rows, step_rows)

    def pair_copies(chunk, tile):
        into = cells.at[part(chunk), tile, pl.ds(col * half_chips, half_chips)]
        own = pltpu.make_async_copy(
            pair_ref.at[tile_rows(chunk, col), :, tile], into, pair_sems.at[0, chunk, tile]
        )
        other = pltpu.make_async_remote_copy(
            src_ref=pair_ref.at[tile_rows(chunk, 1 - col), :, tile],
            dst_ref=into,
            send_sem=pair_sems.at[1, chunk, tile],
            recv_sem=pair_sems.at[2, chunk, tile],
            device_id=sibling,
            device_id_type=MESH,
        )
        return own, other

    def out_copies(chunk, tile):
        to = out_ref.at[tile_rows(chunk, col), :, tile]
        own = pltpu.make_async_copy(
            cells.at[part(chunk), tile, pl.ds(col * half_chips, half_chips)],
            to,
            out_sems.at[0, chunk, tile],
        )
        other = pltpu.make_async_remote_copy(
            src_ref=cells.at[part(chunk), tile, pl.ds((1 - col) * half_chips, half_chips)],
            dst_ref=to,
            send_sem=out_sems.at[1, chunk, tile],
            recv_sem=out_sems.at[2, chunk, tile],
            device_id=sibling,
            device_id_type=MESH,
        )
        return own, other

    def left_copy(chunk, target, source):
        return pltpu.make_async_remote_copy(
            src_ref=first_out.at[target, part(chunk), pl.ds(0, per)],
            dst_ref=left_in.at[pl.ds(source * rows + chunk * step_rows, step_rows)],
            send_sem=left_send.at[chunk, target],
            recv_sem=left_recv.at[chunk, source],
            device_id=place(base_team + target),
            device_id_type=MESH,
        )

    def left_own(chunk):
        return pltpu.make_async_copy(
            first_out.at[seat, part(chunk), pl.ds(0, per)],
            left_in.at[pl.ds(seat * rows + chunk * step_rows, step_rows)],
            own_sems.at[0, chunk],
        )

    def right_copy(chunk, target, source):
        return pltpu.make_async_remote_copy(
            src_ref=first_out.at[target % team, part(chunk), pl.ds(per, per)],
            dst_ref=right_in.at[chunk, pl.ds(source * step_rows, step_rows)],
            send_sem=right_send.at[chunk, target],
            recv_sem=right_recv.at[chunk, source],
            device_id=place(target),
            device_id_type=MESH,
        )

    def right_own(chunk):
        return pltpu.make_async_copy(
            first_out.at[seat, part(chunk), pl.ds(per, per)],
            right_in.at[chunk, pl.ds(me * step_rows, step_rows)],
            own_sems.at[1, chunk],
        )

    def team_copy(out_box, in_box, send, recv, index, target, source):
        return pltpu.make_async_remote_copy(
            src_ref=out_box.at[index, target],
            dst_ref=in_box.at[index, source],
            send_sem=send.at[index, target],
            recv_sem=recv.at[index, source],
            device_id=place(base_team + target),
            device_id_type=MESH,
        )

    back_copy = functools.partial(team_copy, back_out, back_in, back_send, back_recv)

    def second_copy(tile, target, source):
        return pltpu.make_async_remote_copy(
            src_ref=second_out.at[tile, target],
            dst_ref=second_in.at[tile, source],
            send_sem=second_send.at[tile, target],
            recv_sem=second_recv.at[tile, source],
            device_id=place(target),
            device_id_type=MESH,
        )

    def last_copy(group, target, source):
        span = pl.ds(groups[group][0], groups[group][1] - groups[group][0])
        return pltpu.make_async_remote_copy(
            src_ref=last_out.at[target, span],
            dst_ref=last_in.at[source, span],
            send_sem=last_send.at[group, target],
            recv_sem=last_recv.at[group, source],
            device_id=place(target),
            device_id_type=MESH,
        )

    def back_own(tile):
        return pltpu.make_async_copy(
            back_out.at[tile, seat], back_in.at[tile, seat], own_sems.at[2, tile]
        )

    def second_own(tile):
        return pltpu.make_async_copy(
            second_out.at[tile, me], second_in.at[tile, me], own_sems.at[3, tile]
        )

    def last_own_copy(group):
        span = pl.ds(groups[group][0], groups[group][1] - groups[group][0])
        return pltpu.make_async_copy(
            last_out.at[me, span], last_in.at[me, span], last_own.at[group]
        )

    def far(step):
        return (me + step) % owners

    def near(step):
        return (seat + step) % team

    def send_left(chunk):
        left_own(chunk).start()
        each(1, team, lambda step: left_copy(chunk, near(step), seat).start())

    def send_right(chunk):
        def act(step):
            right_copy(chunk, other_team + near(step), me).start()
            right_copy(chunk, base_team + near(step), me).start()

        right_own(chunk).start()
        right_copy(chunk, other_team + seat, me).start()
        each(1, team, act)

    def project(update, flat):
        proj = lax.dot_general(
            turned[update], flat, (((1,), (1,)), ((), ())), preferred_element_type=jnp.float32
        )
        width = proj.shape[0] // 4
        left = sigmoid(proj[width : 2 * width]) * proj[:width]
        right = sigmoid(proj[3 * width :]) * proj[2 * width : 3 * width]
        return left, right

    def mask_at(at):
        chunk, step = at // step_rows, at % step_rows
        return row * (2 * rows) + chunk * (2 * step_rows) + col * step_rows + step

    def produce_first(chunk):
        bias = bias_v[...].astype(jnp.float32)

        def one_row(step):
            at = chunk * step_rows + step
            token = mask_at(at)
            values = cells[at].reshape(tokens, channels).astype(jnp.float32)
            same = chain_v[...] == chain_s[token]
            start = (values + jnp.where(same, bias, 0.0)).astype(jnp.bfloat16)
            cells[at] = start.reshape(tiles, chips, pair_rows, channels)
            flat = normalise(start.astype(jnp.float32), 1)
            normed[at] = flat.reshape(tiles, lanes, channels)
            mask = mask_s[token].astype(jnp.float32) * mask_v[...]
            for side, gated in enumerate(project(0, flat)):
                piece = (mask * gated).astype(jnp.bfloat16).reshape(team, per, tokens)
                first_out[:, at, side * per : (side + 1) * per] = piece

        each(0, step_rows, one_row)

    def widen(block, base):
        block = block.astype(jnp.float32).reshape(-1, block.shape[-1])
        size = block.shape[0]
        for tile in range(block.shape[1] // lanes):
            wide[tile, pl.ds(base, size), :] = block[:, tile * lanes : (tile + 1) * lanes]

    def pick(first, size, stride):
        pieces = [
            wide[tile, pl.ds(first, size, stride=stride), :].astype(jnp.bfloat16)
            for tile in range(tiles)
        ]
        return jnp.concatenate(pieces, axis=1)

    right_base = team_rows * per

    def widen_left(chunk, source):
        first = source * rows + chunk * step_rows
        widen(left_in[pl.ds(first, step_rows)], pl.multiple_of(first * per, per))

    def widen_right(chunk, source):
        first = source * step_rows
        base = pl.multiple_of(right_base + first * per, per)
        widen(right_in[chunk, pl.ds(first, step_rows)], base)

    def take_left():
        for chunk in range(CHUNKS):
            left_own(chunk).wait()
            widen_left(chunk, seat)

            def arrive(step):
                source = (seat + team - step) % team
                left_copy(chunk, seat, source).wait_recv()
                widen_left(chunk, source)

            each(1, team, arrive)

    def take_right(chunk):
        def arrive(step):
            source = (me + owners - step) % owners
            right_copy(chunk, me, source).wait_recv()
            widen_right(chunk, source)

        right_own(chunk).wait()
        widen_right(chunk, me)
        each(1, owners, arrive)

    def contract_first(tile):
        def channel(index):
            left = pick(index, team_rows, per)
            right = pick(right_base + index, lanes, per)
            tri = lax.dot_general(
                left, right, (((1,), (1,)), ((), ())), preferred_element_type=jnp.float32
            )
            products[pl.ds(index, team_rows, stride=per), :] = tri

        each(0, per, channel)
        size = rows * per

        def give(step):
            target = near(step)
            base = pl.multiple_of(target * size, size)
            back_out[tile, target] = products[pl.ds(base, size), :].astype(jnp.bfloat16)

            @pl.when(step > 0)
            def _():
                back_copy(tile, target, seat).start()

        each(0, team, give)
        back_own(tile).start()

    def finish(update, at, tile, tris):
        tri = jnp.concatenate(tris, axis=1)
        here = pl.ds(at, batch)
        change = lax.dot_general(
            normalise(tri, 0),
            outw_v[update],
            (((0,), (0,)), ((), ())),
            preferred_element_type=jnp.float32,
        )
        flat = normed[here, tile].reshape(batch * lanes, channels)
        gating = sigmoid(jnp.dot(flat, gate_v[update], preferred_element_type=jnp.float32))
        values = cells[here, tile].reshape(batch * lanes, channels).astype(jnp.float32)
        result = (values + gating * change).astype(jnp.bfloat16)
        cells[here, tile] = result.reshape(batch, chips, pair_rows, channels)
        return result

    def arrived(copy, index, people, own):
        each(1, people, lambda step: copy(index, own, (own + people - step) % people).wait_recv())

    def consume_first(tile):
        arrived(back_copy, tile, team, seat)
        back_own(tile).wait()
        mask_tile = mask_v[:, tile * lanes : (tile + 1) * lanes]

        def some_rows(step):
            at = step * batch
            tris = []
            for which in range(batch):
                base = pl.multiple_of((at + which) * per, per)
                tri = back_in[tile, :, pl.ds(base, per), :].astype(jnp.float32)
                tris.append(tri.reshape(team * per, lanes))
            result = finish(0, at, tile, tris)
            flat = normalise(result.astype(jnp.float32), 1)
            normed[pl.ds(at, batch), tile] = flat.reshape(batch, lanes, channels)
            left, right = project(1, flat)
            for which in range(batch):
                mask = mask_s[mask_at(at + which)].astype(jnp.float32) * mask_tile
                span = slice(which * lanes, (which + 1) * lanes)
                pieces = [
                    (mask * gated[:, span]).reshape(owners, share, lanes)
                    for gated in (left, right)
                ]
                piece = jnp.concatenate(pieces, axis=1).astype(jnp.bfloat16)
                second_out[tile, :, at + which] = piece

        each(0, rows // batch, some_rows)
        second_own(tile).start()
        each(1, owners, lambda step: second_copy(tile, far(step), me).start())

    def take_second(tile):
        def put(source):
            size = rows * 2 * share
            block = second_in[tile, source].astype(jnp.float32).reshape(size, lanes)
            wide[tile, pl.ds(pl.multiple_of(source * size, size), size), :] = block

        def arrive(step):
            source = (me + owners - step) % owners
            second_copy(tile, me, source).wait_recv()
            put(source)

        second_own(tile).wait()
        put(me)
        each(1, owners, arrive)

    block_size = lanes * share

    def contract_second(newest):
        def channel(index):
            def side(tile, first):
                values = wide[tile, pl.ds(first, tokens, stride=2 * share), :]
                return values.astype(jnp.bfloat16)

            def product(left, right):
                return lax.dot_general(
                    left, right, (((0,), (0,)), ((), ())), preferred_element_type=jnp.float32
                )

            def store(chunk, tile, tri):
                first = blocks.index((chunk, tile)) * block_size
                products[pl.ds(first + index, lanes, stride=share), :] = tri

            lefts = [side(tile, index) for tile in range(newest + 1)]
            rights = [side(tile, share + index) for tile in range(newest + 1)]
            level = product(lefts[newest], jnp.concatenate(rights, axis=1))
            for tile in range(newest + 1):
                store(newest, tile, level[:, tile * lanes : (tile + 1) * lanes])
            if newest:
                upright = product(jnp.concatenate(lefts[:newest], axis=1), rights[newest])
                for chunk in range(newest):
                    store(chunk, newest, upright[chunk * lanes : (chunk + 1) * lanes])

        each(0, share, channel)
        size = step_rows * share
        for group, (first, last, when) in enumerate(groups):
            if when != newest:
                continue

            def give(step):
                target = far(step)
                for block in range(first, last):
                    base = pl.multiple_of(block * block_size + target * size, size)
                    last_out[target, block] = products[pl.ds(base, size), :].astype(jnp.bfloat16)

                @pl.when(step > 0)
                def _():
                    last_copy(group, target, me).start()

            each(0, owners, give)
            last_own_copy(group).start()

    def consume_second(group):
        arrived(last_copy, group, owners, me)
        last_own_copy(group).wait()
        for block in range(groups[group][0], groups[group][1]):
            chunk, tile = blocks[block]
            for first in range(0, step_rows, batch):
                tris = []
                for which in range(first, first + batch, 2):
                    two = last_in[:, block, which * share : (which + 2) * share, :]
                    two = two.astype(jnp.float32)
                    tris.append(two[:, :share].reshape(owners * share, lanes))
                    tris.append(two[:, share:].reshape(owners * share, lanes))
                finish(1, chunk * step_rows + first, tile, tris)
            for copy in out_copies(chunk, tile):
                copy.start()

    grid = [(chunk, tile) for chunk in range(CHUNKS) for tile in range(tiles)]
    for at in grid:
        for copy in pair_copies(*at):
            copy.start()
    for update in range(2):
        turned[update] = proj_v[update].astype(jnp.float32).T.astype(jnp.bfloat16)
    for chunk in range(CHUNKS):
        for tile in range(tiles):
            for copy in pair_copies(chunk, tile):
                copy.wait()
        produce_first(chunk)
        if chunk == 0:
            send_right(0)
        send_left(chunk)
    for chunk in range(1, CHUNKS):
        send_right(chunk)
    take_left()
    for tile in range(tiles):
        take_right(tile)
        contract_first(tile)
        if tile:
            consume_first(tile - 1)
    consume_first(tiles - 1)
    for tile in range(tiles):
        take_second(tile)
        contract_second(tile)
    for group in range(len(groups)):
        consume_second(group)

    for chunk in range(CHUNKS):

        def sent(step):
            left_copy(chunk, near(step), seat).wait_send()
            right_copy(chunk, other_team + near(step), me).wait_send()
            right_copy(chunk, base_team + near(step), me).wait_send()
            back_copy(chunk, near(step), seat).wait_send()

        right_copy(chunk, other_team + seat, me).wait_send()
        each(1, team, sent)
    for tile in range(tiles):
        each(1, owners, lambda step: second_copy(tile, far(step), me).wait_send())
    for group in range(len(groups)):
        each(1, owners, lambda step: last_copy(group, far(step), me).wait_send())
    for at in grid:
        for copy in out_copies(*at):
            copy.wait()


def fused_shards(
    pair, chain_ids, token_mask, same_chain_bias, proj_weight, gate_weight, out_weight
):
    rows_tile, cols_tile, channels = pair.shape
    chips = lax.axis_size("row")
    owners = 2 * chips
    team = owners // 2
    tokens = 2 * cols_tile
    rows = rows_tile // 2
    step_rows = rows // CHUNKS
    hidden = proj_weight.shape[2] // 4
    per = hidden // team
    lanes = owners * step_rows
    share = hidden // owners
    blocks, groups = [len(part) for part in block_order()]

    def dealt(values):
        parts = values.reshape(chips, CHUNKS, 2 * step_rows)
        return parts.transpose(1, 0, 2).reshape(tokens)

    chain_cols = jnp.broadcast_to(dealt(chain_ids)[:, None], (tokens, channels))
    bf16, f32 = jnp.bfloat16, jnp.float32
    vmem = pl.BlockSpec(memory_space=pltpu.VMEM)
    smem = pl.BlockSpec(memory_space=pltpu.SMEM)
    anywhere = pl.BlockSpec(memory_space=pl.ANY)
    view = (rows_tile, chips // 2, CHUNKS, 2 * step_rows, channels)

    def sems(*shape):
        return pltpu.SemaphoreType.DMA(shape)

    result = pl.pallas_call(
        functools.partial(fused_kernel, chips),
        out_shape=jax.ShapeDtypeStruct(view, pair.dtype),
        in_specs=[anywhere, smem, smem, vmem, vmem, vmem, vmem, vmem, vmem],
        out_specs=anywhere,
        scratch_shapes=[
            pltpu.VMEM((2, 4 * hidden, channels), bf16),
            pltpu.VMEM((rows, CHUNKS, chips, 2 * step_rows, channels), bf16),
            pltpu.VMEM((rows, CHUNKS, lanes, channels), bf16),
            pltpu.VMEM((team, rows, 2 * per, tokens), bf16),
            pltpu.VMEM((team * rows, per, tokens), bf16),
            pltpu.VMEM((CHUNKS, lanes, per, tokens), bf16),
            pltpu.VMEM((CHUNKS, team * rows * 2 * per, lanes), f32),
            pltpu.VMEM((blocks * lanes * share, lanes), f32),
            pltpu.VMEM((CHUNKS, team, rows * per, lanes), bf16),
            pltpu.VMEM((CHUNKS, team, rows * per, lanes), bf16),
            pltpu.VMEM((CHUNKS, owners, rows, 2 * share, lanes), bf16),
            pltpu.VMEM((CHUNKS, owners, rows, 2 * share, lanes), bf16),
            pltpu.VMEM((owners, blocks, step_rows * share, lanes), bf16),
            pltpu.VMEM((owners, blocks, step_rows * share, lanes), bf16),
            sems(3, CHUNKS, CHUNKS),
            sems(CHUNKS, team),
            sems(CHUNKS, team),
            sems(CHUNKS, owners),
            sems(CHUNKS, owners),
            sems(CHUNKS, team),
            sems(CHUNKS, team),
            sems(CHUNKS, owners),
            sems(CHUNKS, owners),
            sems(groups, owners),
            sems(groups, owners),
            sems(4, CHUNKS),
            sems(groups),
            sems(3, CHUNKS, CHUNKS),
        ],
        compiler_params=pltpu.CompilerParams(
            collective_id=0, has_side_effects=True, vmem_limit_bytes=60 * 1024 * 1024
        ),
    )(
        pair.reshape(view),
        chain_ids,
        token_mask,
        chain_cols,
        dealt(token_mask).astype(f32)[None, :],
        same_chain_bias[None, :],
        proj_weight,
        gate_weight,
        out_weight,
    )
    return result.reshape(pair.shape)


def fits(pair, proj_weight):
    rows_tile, cols_tile, channels = pair.shape
    rows_grid, cols_grid = lax.axis_size("row"), lax.axis_size("col")
    hidden = proj_weight.shape[2] // 4
    return (
        cols_grid == 2
        and rows_grid % 2 == 0
        and hidden == 8 * cols_grid * rows_grid
        and channels == 128
        and rows_tile % (4 * CHUNKS) == 0
        and cols_tile % 64 == 0
        and rows_tile * rows_grid == 128 * CHUNKS
        and rows_tile * rows_grid == cols_tile * cols_grid
    )


def program_shards(pair, chain_ids, token_mask, same_chain_bias, proj_weight, *rest):
    chosen = fused_shards if fits(pair, proj_weight) else shards
    return chosen(pair, chain_ids, token_mask, same_chain_bias, proj_weight, *rest)


def solution(mesh):
    return jax.shard_map(
        program_shards,
        mesh=mesh,
        in_specs=(P(("group", "row"), "col", None), P("group"), P("group"), P(), P(), P(), P()),
        out_specs=P(("group", "row"), "col", None),
        check_vma=False,
    )
```
